512 devices in a mesh: seq: 64 (over y, z), head: 8 (over x, core).
Axes of the slice: x: 4, y: 4, z: 16, core: 2. Of those that a mesh axis runs over, the one named last changes fastest.
Arguments:
- query_in: bfloat16 [32768, 4096], P('seq', 'head'), may hold values from -128 to 128
- key_in: bfloat16 [32768, 4096], P('seq', 'head'), may hold values from -6 to 6
- value_in: bfloat16 [32768, 4096], P('seq', 'head'), may hold values from -6 to 6
- upstream: bfloat16 [32768, 4096], P('seq', 'head'), may hold values from -24 to 24
- norm_gain: float32 [4096], P('head'), may hold values from 0.1 to 1.9
- state_in: float32 [32, 128, 128], P('head'), may hold values from -96 to 96
Outputs:
- normed_out: bfloat16 [32768, 4096], P('seq', 'head')
- query_grad: bfloat16 [32768, 4096], P('seq', 'head')
- key_grad: bfloat16 [32768, 4096], P('seq', 'head')
- value_grad: bfloat16 [32768, 4096], P('seq', 'head')
- gain_grad: float32 [4096], P('head')
- state_grad: float32 [32, 128, 128], P('head')
The draws below stay inside these ranges and needn't reach their ends.
All inputs are finite; a program needn't handle non-finite values.
Results may differ from the reference program's by a relative error of at most 0.0026.
Values sent between devices are 32-bit elements; how exact they have to be, the bound alone decides.
A program may use at most 128 MiB of HBM per device.

```python
import math
import jax
import jax.numpy as jnp
from jax import lax

HEADS = 32
HEAD = 128
TOK_DEV = 512
WIDTH = 4096
TOKENS = 32768
N_SEQ = 64


def draw_query_in(key, part):
    first, second = jax.random.split(key, 2)
    base = jnp.clip(jax.random.normal(first, (TOKENS, HEADS * HEAD), jnp.float32), -4.0, 4.0)
    rows = jnp.exp(jax.random.uniform(second, (TOKENS, 1), jnp.float32, 0.0, math.log(10.0)))
    head_index = (jnp.arange(HEADS * HEAD) // HEAD).astype(jnp.float32)
    columns = jnp.exp(0.5 * math.log(10.0) * head_index / max(HEADS - 1, 1))
    return (base * rows * columns[None, :]).astype(jnp.bfloat16)


def draw_upstream(key, part):
    first, second = jax.random.split(key, 2)
    base = jnp.clip(jax.random.normal(first, (TOKENS, HEADS * HEAD), jnp.float32), -4.0, 4.0)
    position = jnp.arange(TOKENS).astype(jnp.float32) / max(TOKENS - 1, 1)
    rising = jnp.exp(math.log(3.0) * position)[:, None]
    rows = jnp.exp(jax.random.uniform(second, (TOKENS, 1), jnp.float32, 0.0, math.log(2.0)))
    return (base * rising * rows).astype(jnp.bfloat16)


def levels(key, extent, cuts, smallest, largest):
    factor_of = 1.0
    for dim, parts in cuts:
        draws = jax.random.uniform(jax.random.fold_in(jax.random.fold_in(key, 6), dim), (parts,), jnp.float32, smallest / len(cuts), largest / len(cuts))
        factor_of = factor_of * jnp.repeat(jnp.exp(draws), extent[dim] // parts).reshape((-1,) + (1,) * (len(extent) - 1 - dim))
    return factor_of


def normal_values(own_key, extent, spread, bound, cuts=(), kind=jnp.bfloat16):
    level = levels(own_key, extent, cuts, -0.22, 0.18) if cuts else 1.0
    entries = jax.random.normal(own_key, extent, jnp.float32) * spread * level
    return jnp.minimum(jnp.maximum(entries, -bound), bound).astype(kind)


def setup_inputs(seed: int = 0) -> dict:
    key_of = jax.random.split(jax.random.key(seed), 7)
    query_in = draw_query_in(jax.random.fold_in(key_of[6], 71), 0)
    key_in = normal_values(key_of[1], (TOKENS, WIDTH), 1.0, 6.0, ((0, 64), (1, 8)))
    value_in = normal_values(key_of[2], (TOKENS, WIDTH), 1.0, 6.0, ((0, 64), (1, 8)))
    upstream = draw_upstream(jax.random.fold_in(key_of[6], 71), 0)
    norm_gain = jnp.clip(1.0 + 0.18 * jax.random.normal(key_of[4], (WIDTH,), jnp.float32), 0.1, 1.9)
    state_in = normal_values(key_of[5], (HEADS, HEAD, HEAD), 16.0, 96.0, ((0, 8),), jnp.float32)
    return dict(query_in=query_in, key_in=key_in, value_in=value_in, upstream=upstream, norm_gain=norm_gain, state_in=state_in)


def reference(query_in, key_in, value_in, upstream, norm_gain, state_in):
    block_shape = (N_SEQ, TOK_DEV, HEADS, HEAD)
    queries = query_in.reshape(block_shape)
    keys_all = key_in.reshape(block_shape)
    values_all = value_in.reshape(block_shape)
    causal = jnp.tril(jnp.ones((TOK_DEV, TOK_DEV), dtype=bool))[None]
    highest = lax.Precision.HIGHEST

    def block_scores(query_rows, key_rows):
        raw = jnp.einsum('thd,shd->hts', query_rows.astype(jnp.float32), key_rows.astype(jnp.float32))
        return jnp.where(causal, raw, 0.0).astype(jnp.bfloat16)

    def forward_step(running, pieces):
        query_rows, key_rows, value_rows = pieces
        scores = block_scores(query_rows, key_rows)
        inside = jnp.einsum('hts,she->the', scores.astype(jnp.float32), value_rows.astype(jnp.float32))
        carried = jnp.einsum('thd,hde->the', query_rows.astype(jnp.float32), running, precision=highest)
        grown = running + jnp.einsum('thd,the->hde', key_rows.astype(jnp.float32), value_rows.astype(jnp.float32))
        return (grown, (inside + carried, running))
    final_state, (attended, befores) = lax.scan(forward_step, state_in, (queries, keys_all, values_all))
    flattened = attended.reshape(TOKENS, WIDTH)
    mean_square = lax.optimization_barrier(jnp.mean(flattened * flattened, axis=1, keepdims=True))
    inverse = lax.rsqrt(mean_square + 1e-06)
    normed = flattened * inverse
    normed_out = (normed * norm_gain).astype(jnp.bfloat16)
    upstream_full = upstream.astype(jnp.float32)
    scaled = upstream_full * norm_gain
    product = lax.optimization_barrier(jnp.mean(scaled * flattened, axis=1, keepdims=True))
    d_full = inverse * (scaled - flattened * (product * inverse * inverse))
    gain_grad = lax.optimization_barrier(jnp.sum(upstream_full * normed, axis=0))
    d_low = d_full.astype(jnp.bfloat16)

    def backward_step(suffix, pieces):
        query_rows, key_rows, value_rows, full_rows, low_rows, running = pieces
        scores = block_scores(query_rows, key_rows)
        d_raw = jnp.einsum('the,she->hts', low_rows.astype(jnp.float32), value_rows.astype(jnp.float32))
        d_scores = jnp.where(causal, d_raw, 0.0).astype(jnp.bfloat16)
        query_part = jnp.einsum('hts,shd->thd', d_scores.astype(jnp.float32), key_rows.astype(jnp.float32))
        query_part = query_part + jnp.einsum('the,hde->thd', full_rows, running, precision=highest)
        key_part = jnp.einsum('hts,thd->shd', d_scores.astype(jnp.float32), query_rows.astype(jnp.float32))
        key_part = key_part + jnp.einsum('she,hde->shd', value_rows.astype(jnp.float32), suffix, precision=highest)
        value_part = jnp.einsum('hts,the->she', scores.astype(jnp.float32), low_rows.astype(jnp.float32))
        value_part = value_part + jnp.einsum('shd,hde->she', key_rows.astype(jnp.float32), suffix, precision=highest)
        grown = suffix + jnp.einsum('thd,the->hde', query_rows.astype(jnp.float32), low_rows.astype(jnp.float32))
        return (grown, (query_part.astype(jnp.bfloat16), key_part.astype(jnp.bfloat16), value_part.astype(jnp.bfloat16)))
    inputs_back = (queries, keys_all, values_all, d_full.reshape(block_shape), d_low.reshape(block_shape), befores)
    start_grad = jnp.zeros((HEADS, HEAD, HEAD), jnp.float32)
    state_grad, (query_grad, key_grad, value_grad) = lax.scan(backward_step, start_grad, inputs_back, reverse=True)
    return (normed_out, query_grad.reshape(TOKENS, WIDTH), key_grad.reshape(TOKENS, WIDTH), value_grad.reshape(TOKENS, WIDTH), gain_grad, state_grad)
```

```python
import functools

import jax
import jax.numpy as jnp
from jax import lax
from jax.experimental import pallas as pl
from jax.experimental.pallas import tpu as pltpu
from jax.sharding import PartitionSpec as P

F32 = jnp.float32
BF16 = jnp.bfloat16
MESH = pl.DeviceIdType.MESH
HEAD = 128
ROWS = 8
PLANES = 16
LINES = 4


def nn(a, b):
    return lax.dot_general(a, b, (((1,), (0,)), ((), ())), preferred_element_type=F32)


def nt(a, b):
    return lax.dot_general(a, b, (((1,), (1,)), ((), ())), preferred_element_type=F32)


def tn(a, b):
    return lax.dot_general(a, b, (((0,), (0,)), ((), ())), preferred_element_type=F32)


def halves(x):
    high = x.astype(BF16)
    return high, (x - high.astype(F32)).astype(BF16)


def copy_to(src, dst, send, recv, **where):
    return pltpu.make_async_remote_copy(
        src, dst, send, recv, device_id=where, device_id_type=MESH
    )


def kernel(
    q_in, k_in, v_in, u_in, gain_ref, state_ref,
    normed_out, qgrad_out, kgrad_out, vgrad_out, gain_out, state_out,
    q, k, v, u, qt, att, dfull, dlow, kpart, vpart,
    normed_buf, qgrad_buf, kgrad_buf, vgrad_buf,
    local1, got1, part1, before, local2, got2, part2, after,
    stats, own_row, rows,
    in_sem, out_sem, send_sem, recv_sem,
):
    n_seq = lax.axis_size("seq")
    n_head = lax.axis_size("head")
    me = lax.axis_index("seq")
    mine = lax.axis_index("head")
    plane = lax.rem(me, PLANES)
    line = me // PLANES
    tokens = q.shape[0]
    heads = q.shape[1] // HEAD
    half = tokens // 2

    loads = [
        pltpu.make_async_copy(src, dst, in_sem.at[i])
        for i, (src, dst) in enumerate(((k_in, k), (v_in, v), (q_in, q), (u_in, u)))
    ]
    for load in loads:
        load.start()

    def step_z(j):
        far = (j + 1) // 2
        away = PLANES // 2 + jnp.where(lax.rem(j, 2) == 1, -far, far)
        return lax.rem(plane + away, PLANES)

    def each_seq(act):
        def body(j, carry):
            z = step_z(j)
            for dy in (2, 1, 3, 0):
                act(lax.rem(line + dy, LINES) * PLANES + z)
            return carry

        lax.fori_loop(0, PLANES - 1, body, 0)
        for dy in (2, 1, 3):
            act(lax.rem(line + dy, LINES) * PLANES + plane)

    barrier = pltpu.get_barrier_semaphore()
    each_seq(
        lambda d: pl.semaphore_signal(barrier, inc=1, device_id={"seq": d}, device_id_type=MESH)
    )
    for i in range(1, n_head):
        pl.semaphore_signal(
            barrier, inc=1, device_id={"head": lax.rem(mine + i, n_head)}, device_id_type=MESH
        )

    def cols(h):
        return slice(h * HEAD, (h + 1) * HEAD)

    def lower(x):
        r = lax.broadcasted_iota(jnp.int32, x.shape, 0)
        c = lax.broadcasted_iota(jnp.int32, x.shape, 1)
        return r >= c

    def upper(x):
        r = lax.broadcasted_iota(jnp.int32, x.shape, 0)
        c = lax.broadcasted_iota(jnp.int32, x.shape, 1)
        return r <= c

    lo, hi = slice(0, half), slice(half, tokens)

    def causal(a, b, c):
        s = nt(a[lo], b[lo])
        top = nn(jnp.where(lower(s), s, 0.0).astype(BF16), c[lo])
        s = nt(a[hi], b[hi])
        low = nn(jnp.where(lower(s), s, 0.0).astype(BF16), c[hi])
        low = low + nn(nt(a[hi], b[lo]).astype(BF16), c[lo])
        return top, low

    def anticausal(a, b, c):
        s = nt(a[hi], b[hi])
        low = nn(jnp.where(upper(s), s, 0.0).astype(BF16), c[hi])
        s = nt(a[lo], b[lo])
        top = nn(jnp.where(upper(s), s, 0.0).astype(BF16), c[lo])
        top = top + nn(nt(a[lo], b[hi]).astype(BF16), c[hi])
        return top, low

    loads[0].wait()
    loads[1].wait()
    for h in range(heads):
        kv = tn(k[:, cols(h)], v[:, cols(h)])
        local1[h * PLANES : (h + 1) * PLANES] = kv.reshape(PLANES, ROWS, HEAD)
    loads[2].wait()
    loads[3].wait()

    def forward_inside(h):
        top, low = causal(q[:, cols(h)], k[:, cols(h)], v[:, cols(h)])
        att[lo, cols(h)] = top
        att[hi, cols(h)] = low

    forward_inside(0)
    pl.semaphore_wait(barrier, n_seq - 1 + n_head - 1)

    def all_but_one(ref):
        return ref.at[pl.ds(0, n_seq - 1)]

    def scatter(local, got, sems):
        each_seq(
            lambda d: copy_to(
                local.at[d], got.at[me], send_sem.at[sems], recv_sem.at[sems], seq=d
            ).start()
        )
        got[me] = local[me]

    def arrived(ref, sems):
        ref = all_but_one(ref)
        copy_to(ref, ref, send_sem.at[sems], recv_sem.at[sems], seq=me).wait_recv()

    def sent(ref, sems):
        ref = all_but_one(ref)
        copy_to(ref, ref, send_sem.at[sems], recv_sem.at[sems], seq=me).wait_send()

    scatter(local1, got1, 0)
    forward_inside(1)
    for h in range(heads):
        qt[h] = q[:, cols(h)].T
    arrived(got1, 0)
    total = state_ref[me]
    for b in range(n_seq):
        part1[b] = total
        total = total + got1[b]
    scatter(part1, before, 1)
    for h in range(2, heads):
        forward_inside(h)
    arrived(before, 1)

    def state_of(ref, h):
        return ref[h * PLANES : (h + 1) * PLANES].reshape(HEAD, HEAD)

    def gain_of(h):
        return gain_ref[h : h + 1, :]

    squares = jnp.zeros((tokens, HEAD), F32)
    products = jnp.zeros((tokens, HEAD), F32)
    for h in range(heads):
        high, low = halves(state_of(before, h))
        qh = q[:, cols(h)]
        a = att[:, cols(h)] + (nn(qh, high) + nn(qh, low))
        att[:, cols(h)] = a
        squares = squares + a * a
        products = products + a * (u[:, cols(h)].astype(F32) * gain_of(h))
    blocks = tokens // HEAD
    for j in range(blocks):
        rows_j = slice(j * HEAD, (j + 1) * HEAD)
        stats[mine, j : j + 1, :] = jnp.sum(squares[rows_j].T, axis=0, keepdims=True)
        stats[mine, blocks + j : blocks + j + 1, :] = jnp.sum(
            products[rows_j].T, axis=0, keepdims=True
        )
    for i in range(1, n_head):
        copy_to(
            stats.at[mine], stats.at[mine], send_sem.at[2], recv_sem.at[2],
            head=lax.rem(mine + i, n_head),
        ).start()
    others = stats.at[pl.ds(0, n_head - 1)]
    copy_to(others, others, send_sem.at[2], recv_sem.at[2], head=mine).wait_recv()
    total = stats[0]
    for i in range(1, n_head):
        total = total + stats[i]
    mean = total * (1.0 / (heads * HEAD * n_head))
    inverse = lax.rsqrt(mean[:blocks] + 1e-06)
    coef = mean[blocks:] * inverse * inverse

    def column(x, j):
        return jnp.broadcast_to(x[j : j + 1, :], (HEAD, HEAD)).T

    inverse = jnp.concatenate([column(inverse, j) for j in range(blocks)], axis=0)
    coef = jnp.concatenate([column(coef, j) for j in range(blocks)], axis=0)
    for h in range(heads):
        scaled = u[:, cols(h)].astype(F32) * gain_of(h)
        d = inverse * (scaled - att[:, cols(h)] * coef)
        d_low = d.astype(BF16)
        dfull[:, cols(h)] = d
        dlow[:, cols(h)] = d_low
        local2[h * PLANES : (h + 1) * PLANES] = nn(qt[h], d_low).reshape(PLANES, ROWS, HEAD)
    scatter(local2, got2, 3)

    own_row[1] = jnp.zeros((ROWS, HEAD), F32)
    for h in range(heads):
        normed = att[:, cols(h)] * inverse
        normed_buf[:, cols(h)] = (normed * gain_of(h)).astype(BF16)
        own_row[1, h : h + 1, :] = jnp.sum(
            u[:, cols(h)].astype(F32) * normed, axis=0, keepdims=True
        )
    stores = [pltpu.make_async_copy(normed_buf, normed_out, out_sem.at[0])]
    stores[0].start()

    def query_gradient(h):
        d_low = dlow[:, cols(h)]
        d_rest = (dfull[:, cols(h)] - d_low.astype(F32)).astype(BF16)
        high, low = halves(state_of(before, h))
        carried = nt(d_low, high) + (nt(d_low, low) + nt(d_rest, high))
        top, low = causal(d_low, v[:, cols(h)], k[:, cols(h)])
        qgrad_buf[lo, cols(h)] = (top + carried[lo]).astype(BF16)
        qgrad_buf[hi, cols(h)] = (low + carried[hi]).astype(BF16)

    for h in range(heads):
        query_gradient(h)
    stores.append(pltpu.make_async_copy(qgrad_buf, qgrad_out, out_sem.at[1]))
    stores[1].start()

    arrived(got2, 3)
    total = jnp.zeros((ROWS, HEAD), F32)
    for b in reversed(range(n_seq)):
        part2[b] = total
        total = total + got2[b]
    own_row[0] = total
    scatter(part2, after, 4)

    def along_z(j):
        far = (j + 1) // 2
        return step_z(j)

    def send_row(j, carry):
        z = step_z(j)
        copy_to(
            own_row, rows.at[line, pl.ds(2 * plane, 2)], send_sem.at[5], recv_sem.at[5],
            seq=line * PLANES + z,
        ).start()
        return carry

    lax.fori_loop(0, PLANES - 1, send_row, 0)
    rows[line, pl.ds(2 * plane, 2)] = own_row[...]

    for h in range(heads):
        top, low = anticausal(v[:, cols(h)], dlow[:, cols(h)], q[:, cols(h)])
        kpart[lo, cols(h)] = top
        kpart[hi, cols(h)] = low
        top, low = anticausal(k[:, cols(h)], q[:, cols(h)], dlow[:, cols(h)])
        vpart[lo, cols(h)] = top
        vpart[hi, cols(h)] = low

    some = rows.at[0, pl.ds(0, 2 * (PLANES - 1))]
    copy_to(some, some, send_sem.at[5], recv_sem.at[5], seq=me).wait_recv()
    for i in (2, 1, 3):
        copy_to(
            rows.at[line], rows.at[line], send_sem.at[6], recv_sem.at[6],
            seq=lax.rem(line + i, LINES) * PLANES + plane,
        ).start()

    arrived(after, 4)
    for h in range(heads):
        high, low = halves(state_of(after, h))
        vh, kh = v[:, cols(h)], k[:, cols(h)]
        kgrad_buf[:, cols(h)] = (kpart[:, cols(h)] + (nt(vh, high) + nt(vh, low))).astype(BF16)
        vgrad_buf[:, cols(h)] = (vpart[:, cols(h)] + (nn(kh, high) + nn(kh, low))).astype(BF16)
    stores.append(pltpu.make_async_copy(kgrad_buf, kgrad_out, out_sem.at[2]))
    stores.append(pltpu.make_async_copy(vgrad_buf, vgrad_out, out_sem.at[3]))
    stores[2].start()
    stores[3].start()

    some = rows.at[pl.ds(0, LINES - 1)]
    copy_to(some, some, send_sem.at[6], recv_sem.at[6], seq=me).wait_recv()
    gain = jnp.zeros((ROWS, HEAD), F32)
    for y in range(LINES):
        for z in range(PLANES):
            state_out[y * PLANES + z] = rows[y, 2 * z]
            gain = gain + rows[y, 2 * z + 1]
    gain_out[...] = gain[:heads]

    for store in stores:
        store.wait()
    sent(local1, 0)
    sent(part1, 1)
    copy_to(others, others, send_sem.at[2], recv_sem.at[2], head=mine).wait_send()
    sent(local2, 3)
    sent(part2, 4)
    some = rows.at[0, pl.ds(0, 2 * (PLANES - 1))]
    copy_to(some, some, send_sem.at[5], recv_sem.at[5], seq=me).wait_send()
    some = rows.at[pl.ds(0, LINES - 1)]
    copy_to(some, some, send_sem.at[6], recv_sem.at[6], seq=me).wait_send()


def per_device(query_in, key_in, value_in, upstream, norm_gain, state_in):
    tokens, columns = query_in.shape
    heads = state_in.shape[0]
    n_seq = lax.axis_size("seq")
    n_head = lax.axis_size("head")
    wide = jax.ShapeDtypeStruct((tokens, columns), BF16)
    slices = (n_seq, ROWS, HEAD)
    vmem = pl.BlockSpec(memory_space=pltpu.VMEM)
    anywhere = pl.BlockSpec(memory_space=pl.ANY)
    low = pltpu.VMEM((tokens, columns), BF16)
    full = pltpu.VMEM((tokens, columns), F32)
    outs = pl.pallas_call(
        kernel,
        name="attention_and_gradients",
        out_shape=(
            wide, wide, wide, wide,
            jax.ShapeDtypeStruct((heads, HEAD), F32),
            jax.ShapeDtypeStruct(slices, F32),
        ),
        in_specs=[anywhere] * 4 + [vmem] * 2,
        out_specs=[anywhere] * 4 + [vmem] * 2,
        scratch_shapes=[low] * 4
        + [pltpu.VMEM((heads, HEAD, tokens), BF16), full, full, low, full, full]
        + [low] * 4
        + [pltpu.VMEM(slices, F32)] * 8
        + [
            pltpu.VMEM((n_head, ROWS, HEAD), F32),
            pltpu.VMEM((2, ROWS, HEAD), F32),
            pltpu.VMEM((LINES, 2 * PLANES, ROWS, HEAD), F32),
            pltpu.SemaphoreType.DMA((4,)),
            pltpu.SemaphoreType.DMA((4,)),
            pltpu.SemaphoreType.DMA((7,)),
            pltpu.SemaphoreType.DMA((7,)),
        ],
        compiler_params=pltpu.CompilerParams(
            collective_id=0, has_side_effects=True, vmem_limit_bytes=40 << 20
        ),
    )(
        query_in, key_in, value_in, upstream,
        norm_gain.reshape(heads, HEAD), state_in.reshape(slices),
    )
    return (
        outs[0], outs[1], outs[2], outs[3],
        outs[4].reshape(heads * HEAD), outs[5].reshape(state_in.shape),
    )


def solution(mesh):
    wide = P("seq", "head")
    return jax.shard_map(
        per_device,
        mesh=mesh,
        in_specs=(wide, wide, wide, wide, P("head"), P("head", None, None)),
        out_specs=(wide, wide, wide, wide, P("head"), P("head", None, None)),
        check_vma=False,
    )
```

```python
import functools

import jax
import jax.numpy as jnp
from jax import lax
from jax.experimental import pallas as pl
from jax.experimental.pallas import tpu as pltpu
from jax.sharding import PartitionSpec as P

F32 = jnp.float32
BF16 = jnp.bfloat16
MESH = pl.DeviceIdType.MESH
HEAD = 128
ROWS = 8
PLANES = 16
LINES = 4


def nn(a, b):
    return lax.dot_general(a, b, (((1,), (0,)), ((), ())), preferred_element_type=F32)


def nt(a, b):
    return lax.dot_general(a, b, (((1,), (1,)), ((), ())), preferred_element_type=F32)


def tn(a, b):
    return lax.dot_general(a, b, (((0,), (0,)), ((), ())), preferred_element_type=F32)


def halves(x):
    high = x.astype(BF16)
    return high, (x - high.astype(F32)).astype(BF16)


def copy_to(src, dst, send, recv, **where):
    return pltpu.make_async_remote_copy(
        src, dst, send, recv, device_id=where, device_id_type=MESH
    )


def kernel(
    q_in, k_in, v_in, u_in, gain_in, state_in,
    normed_out, qgrad_out, kgrad_out, vgrad_out, gain_out, state_out,
    q, k, v, u, gain_ref, state_ref, qt, att, dfull, dlow, kpart, vpart,
    local1, got1, part1, before, local2, got2, part2, after,
    stats, totals, gains, gains_got,
    in_sem, send_sem, recv_sem,
):
    n_seq = lax.axis_size("seq")
    n_head = lax.axis_size("head")
    me = lax.axis_index("seq")
    mine = lax.axis_index("head")
    plane = lax.rem(me, PLANES)
    line = me // PLANES
    tokens = q.shape[0]
    heads = q.shape[1] // HEAD
    half = tokens // 2

    loads = [
        pltpu.make_async_copy(src, dst, in_sem.at[i])
        for i, (src, dst) in enumerate(
            (
                (k_in, k), (v_in, v), (q_in, q),
                (u_in, u), (gain_in, gain_ref), (state_in, state_ref),
            )
        )
    ]
    for load in loads:
        load.start()

    def step_z(j):
        far = (j + 1) // 2
        away = PLANES // 2 + jnp.where(lax.rem(j, 2) == 1, -far, far)
        return lax.rem(plane + away, PLANES)

    def each_seq(act):
        def body(j, carry):
            z = step_z(j)
            for dy in (2, 1, 3, 0):
                act(lax.rem(line + dy, LINES) * PLANES + z)
            return carry

        lax.fori_loop(0, PLANES - 1, body, 0)
        for dy in (2, 1, 3):
            act(lax.rem(line + dy, LINES) * PLANES + plane)

    barrier = pltpu.get_barrier_semaphore()
    each_seq(
        lambda d: pl.semaphore_signal(barrier, inc=1, device_id={"seq": d}, device_id_type=MESH)
    )
    for i in range(1, n_head):
        pl.semaphore_signal(
            barrier, inc=1, device_id={"head": lax.rem(mine + i, n_head)}, device_id_type=MESH
        )

    def cols(h):
        return slice(h * HEAD, (h + 1) * HEAD)

    def lower(x):
        r = lax.broadcasted_iota(jnp.int32, x.shape, 0)
        c = lax.broadcasted_iota(jnp.int32, x.shape, 1)
        return r >= c

    def upper(x):
        r = lax.broadcasted_iota(jnp.int32, x.shape, 0)
        c = lax.broadcasted_iota(jnp.int32, x.shape, 1)
        return r <= c

    lo, hi = slice(0, half), slice(half, tokens)

    def causal(a, b, c):
        s = nt(a[lo], b[lo])
        top = nn(jnp.where(lower(s), s, 0.0).astype(BF16), c[lo])
        s = nt(a[hi], b[hi])
        low = nn(jnp.where(lower(s), s, 0.0).astype(BF16), c[hi])
        low = low + nn(nt(a[hi], b[lo]).astype(BF16), c[lo])
        return top, low

    def anticausal(a, b, c):
        s = nt(a[hi], b[hi])
        low = nn(jnp.where(upper(s), s, 0.0).astype(BF16), c[hi])
        s = nt(a[lo], b[lo])
        top = nn(jnp.where(upper(s), s, 0.0).astype(BF16), c[lo])
        top = top + nn(nt(a[lo], b[hi]).astype(BF16), c[hi])
        return top, low

    loads[0].wait()
    loads[1].wait()
    for h in range(heads):
        kv = tn(k[:, cols(h)], v[:, cols(h)])
        local1[h * PLANES : (h + 1) * PLANES] = kv.reshape(PLANES, ROWS, HEAD)
    for load in loads[2:]:
        load.wait()

    def forward_inside(h):
        top, low = causal(q[:, cols(h)], k[:, cols(h)], v[:, cols(h)])
        att[lo, cols(h)] = top
        att[hi, cols(h)] = low

    forward_inside(0)
    pl.semaphore_wait(barrier, n_seq - 1 + n_head - 1)

    def all_but_one(ref):
        return ref.at[pl.ds(0, n_seq - 1)]

    def scatter(local, got, sems):
        each_seq(
            lambda d: copy_to(
                local.at[d], got.at[me], send_sem.at[sems], recv_sem.at[sems], seq=d
            ).start()
        )
        got[me] = local[me]

    def arrived(ref, sems):
        ref = all_but_one(ref)
        copy_to(ref, ref, send_sem.at[sems], recv_sem.at[sems], seq=me).wait_recv()

    def sent(ref, sems):
        ref = all_but_one(ref)
        copy_to(ref, ref, send_sem.at[sems], recv_sem.at[sems], seq=me).wait_send()

    scatter(local1, got1, 0)
    forward_inside(1)
    for h in range(heads):
        qt[h] = q[:, cols(h)].T
    arrived(got1, 0)
    total = state_ref[me]
    for b in range(n_seq):
        part1[b] = total
        total = total + got1[b]
    scatter(part1, before, 1)
    for h in range(2, heads):
        forward_inside(h)
    arrived(before, 1)

    def state_of(ref, h):
        return ref[h * PLANES : (h + 1) * PLANES].reshape(HEAD, HEAD)

    def gain_of(h):
        return gain_ref[h : h + 1, :]

    squares = jnp.zeros((tokens, HEAD), F32)
    products = jnp.zeros((tokens, HEAD), F32)
    for h in range(heads):
        high, low = halves(state_of(before, h))
        qh = q[:, cols(h)]
        a = att[:, cols(h)] + (nn(qh, high) + nn(qh, low))
        att[:, cols(h)] = a
        squares = squares + a * a
        products = products + a * (u[:, cols(h)].astype(F32) * gain_of(h))
    blocks = tokens // HEAD
    for j in range(blocks):
        rows_j = slice(j * HEAD, (j + 1) * HEAD)
        stats[mine, j : j + 1, :] = jnp.sum(squares[rows_j].T, axis=0, keepdims=True)
        stats[mine, blocks + j : blocks + j + 1, :] = jnp.sum(
            products[rows_j].T, axis=0, keepdims=True
        )
    for i in range(1, n_head):
        copy_to(
            stats.at[mine], stats.at[mine], send_sem.at[2], recv_sem.at[2],
            head=lax.rem(mine + i, n_head),
        ).start()
    others = stats.at[pl.ds(0, n_head - 1)]
    copy_to(others, others, send_sem.at[2], recv_sem.at[2], head=mine).wait_recv()
    total = stats[0]
    for i in range(1, n_head):
        total = total + stats[i]
    mean = total * (1.0 / (heads * HEAD * n_head))
    inverse = lax.rsqrt(mean[:blocks] + 1e-06)
    coef = mean[blocks:] * inverse * inverse

    def column(x, j):
        return jnp.broadcast_to(x[j : j + 1, :], (HEAD, HEAD)).T

    inverse = jnp.concatenate([column(inverse, j) for j in range(blocks)], axis=0)
    coef = jnp.concatenate([column(coef, j) for j in range(blocks)], axis=0)
    for h in range(heads):
        scaled = u[:, cols(h)].astype(F32) * gain_of(h)
        d = inverse * (scaled - att[:, cols(h)] * coef)
        d_low = d.astype(BF16)
        dfull[:, cols(h)] = d
        dlow[:, cols(h)] = d_low
        local2[h * PLANES : (h + 1) * PLANES] = nn(qt[h], d_low).reshape(PLANES, ROWS, HEAD)
    scatter(local2, got2, 3)

    gains[0] = jnp.zeros((ROWS, HEAD), F32)
    for h in range(heads):
        normed = att[:, cols(h)] * inverse
        normed_out[:, cols(h)] = (normed * gain_of(h)).astype(BF16)
        gains[0, h : h + 1, :] = jnp.sum(
            u[:, cols(h)].astype(F32) * normed, axis=0, keepdims=True
        )

    def partner(i):
        step = (1, 2, 4, 8, 1, 2)[i]
        near = plane if i < 4 else line
        other = near + step - 2 * step * lax.rem(near // step, 2)
        return line * PLANES + other if i < 4 else other * PLANES + plane

    def gain_copy(i):
        return copy_to(
            gains.at[i], gains_got.at[i], send_sem.at[7 + i], recv_sem.at[7 + i], seq=partner(i)
        )

    def gain_step(i):
        gain_copy(i).wait_recv()
        gains[i + 1] = gains[i] + gains_got[i]
        if i < 5:
            gain_copy(i + 1).start()

    gain_copy(0).start()

    def query_gradient(h):
        d_low = dlow[:, cols(h)]
        d_rest = (dfull[:, cols(h)] - d_low.astype(F32)).astype(BF16)
        high, low = halves(state_of(before, h))
        carried = nt(d_low, high) + (nt(d_low, low) + nt(d_rest, high))
        top, low = causal(d_low, v[:, cols(h)], k[:, cols(h)])
        qgrad_out[lo, cols(h)] = (top + carried[lo]).astype(BF16)
        qgrad_out[hi, cols(h)] = (low + carried[hi]).astype(BF16)

    for h in range(heads):
        query_gradient(h)
        if h == 1:
            gain_step(0)
    gain_step(1)

    arrived(got2, 3)
    total = jnp.zeros((ROWS, HEAD), F32)
    for b in reversed(range(n_seq)):
        part2[b] = total
        total = total + got2[b]
    totals[me] = total

    def send_total(j, carry):
        copy_to(
            totals.at[me], totals.at[me], send_sem.at[5], recv_sem.at[5],
            seq=line * PLANES + step_z(j),
        ).start()
        return carry

    lax.fori_loop(0, PLANES - 1, send_total, 0)
    scatter(part2, after, 4)

    for h in range(heads):
        top, low = anticausal(v[:, cols(h)], dlow[:, cols(h)], q[:, cols(h)])
        kpart[lo, cols(h)] = top
        kpart[hi, cols(h)] = low
        top, low = anticausal(k[:, cols(h)], q[:, cols(h)], dlow[:, cols(h)])
        vpart[lo, cols(h)] = top
        vpart[hi, cols(h)] = low

    row = totals.at[pl.ds(line * PLANES, PLANES)]
    some = totals.at[pl.ds(0, PLANES - 1)]
    copy_to(some, some, send_sem.at[5], recv_sem.at[5], seq=me).wait_recv()
    for i in (2, 1, 3):
        copy_to(
            row, row, send_sem.at[6], recv_sem.at[6],
            seq=lax.rem(line + i, LINES) * PLANES + plane,
        ).start()
    gain_step(2)

    arrived(after, 4)
    for h in range(heads):
        high, low = halves(state_of(after, h))
        vh, kh = v[:, cols(h)], k[:, cols(h)]
        kgrad_out[:, cols(h)] = (kpart[:, cols(h)] + (nt(vh, high) + nt(vh, low))).astype(BF16)
        vgrad_out[:, cols(h)] = (vpart[:, cols(h)] + (nn(kh, high) + nn(kh, low))).astype(BF16)

    gain_step(3)
    three = totals.at[pl.ds(0, (LINES - 1) * PLANES)]
    copy_to(three, three, send_sem.at[6], recv_sem.at[6], seq=me).wait_recv()
    state_out[...] = totals[...]
    gain_step(4)
    gain_step(5)
    gain_out[...] = gains[6, :heads, :]

    sent(local1, 0)
    sent(part1, 1)
    copy_to(others, others, send_sem.at[2], recv_sem.at[2], head=mine).wait_send()
    sent(local2, 3)
    sent(part2, 4)
    copy_to(some, some, send_sem.at[5], recv_sem.at[5], seq=me).wait_send()
    copy_to(three, three, send_sem.at[6], recv_sem.at[6], seq=me).wait_send()
    for i in range(6):
        gain_copy(i).wait_send()


def store_kernel(*refs):
    n = len(refs) // 2
    stores = [pltpu.make_async_copy(refs[i], refs[n + i], refs[-1].at[i]) for i in range(n)]
    for store in stores:
        store.start()
    for store in stores:
        store.wait()


def per_device(query_in, key_in, value_in, upstream, norm_gain, state_in):
    tokens, columns = query_in.shape
    heads = state_in.shape[0]
    n_seq = lax.axis_size("seq")
    n_head = lax.axis_size("head")
    wide = jax.ShapeDtypeStruct((tokens, columns), BF16)
    slices = (n_seq, ROWS, HEAD)
    vmem = pl.BlockSpec(memory_space=pltpu.VMEM)
    anywhere = pl.BlockSpec(memory_space=pl.ANY)
    hbm = pl.BlockSpec(memory_space=pltpu.HBM)
    low = pltpu.VMEM((tokens, columns), BF16)
    full = pltpu.VMEM((tokens, columns), F32)
    shapes = (
        wide, wide, wide, wide,
        jax.ShapeDtypeStruct((heads, HEAD), F32),
        jax.ShapeDtypeStruct(slices, F32),
    )
    outs = pl.pallas_call(
        kernel,
        name="attention_and_gradients",
        out_shape=shapes,
        in_specs=[hbm] * 6,
        out_specs=[vmem] * 6,
        scratch_shapes=[low] * 4
        + [pltpu.VMEM((heads, HEAD), F32), pltpu.VMEM(slices, F32)]
        + [pltpu.VMEM((heads, HEAD, tokens), BF16), full, full, low, full, full]
        + [pltpu.VMEM(slices, F32)] * 8
        + [
            pltpu.VMEM((n_head, ROWS, HEAD), F32),
            pltpu.VMEM(slices, F32),
            pltpu.VMEM((7, ROWS, HEAD), F32),
            pltpu.VMEM((6, ROWS, HEAD), F32),
            pltpu.SemaphoreType.DMA((6,)),
            pltpu.SemaphoreType.DMA((13,)),
            pltpu.SemaphoreType.DMA((13,)),
        ],
        compiler_params=pltpu.CompilerParams(
            collective_id=0, has_side_effects=True, vmem_limit_bytes=51 << 20
        ),
    )(
        query_in, key_in, value_in, upstream,
        norm_gain.reshape(heads, HEAD), state_in.reshape(slices),
    )
    outs = pl.pallas_call(
        store_kernel,
        name="store",
        out_shape=shapes,
        in_specs=[anywhere] * 6,
        out_specs=[hbm] * 6,
        scratch_shapes=[pltpu.SemaphoreType.DMA((6,))],
        compiler_params=pltpu.CompilerParams(vmem_limit_bytes=1 << 20),
    )(*outs)
    return (
        outs[0], outs[1], outs[2], outs[3],
        outs[4].reshape(heads * HEAD), outs[5].reshape(state_in.shape),
    )


def solution(mesh):
    wide = P("seq", "head")
    return jax.shard_map(
        per_device,
        mesh=mesh,
        in_specs=(wide, wide, wide, wide, P("head"), P("head", None, None)),
        out_specs=(wide, wide, wide, wide, P("head"), P("head", None, None)),
        check_vma=False,
    )
```

```python
import functools

import jax
import jax.numpy as jnp
from jax import lax
from jax.experimental import pallas as pl
from jax.experimental.pallas import tpu as pltpu
from jax.sharding import PartitionSpec as P

F32 = jnp.float32
BF16 = jnp.bfloat16
MESH = pl.DeviceIdType.MESH
HEAD = 128
ROWS = 8
PLANES = 16
LINES = 4


def nn(a, b):
    return lax.dot_general(a, b, (((1,), (0,)), ((), ())), preferred_element_type=F32)


def nt(a, b):
    return lax.dot_general(a, b, (((1,), (1,)), ((), ())), preferred_element_type=F32)


def tn(a, b):
    return lax.dot_general(a, b, (((0,), (0,)), ((), ())), preferred_element_type=F32)


def halves(x):
    high = x.astype(BF16)
    return high, (x - high.astype(F32)).astype(BF16)


def copy_to(src, dst, send, recv, **where):
    return pltpu.make_async_remote_copy(
        src, dst, send, recv, device_id=where, device_id_type=MESH
    )


def kernel(
    q_in, k_in, v_in, u_in, gain_in, state_in,
    normed_out, qgrad_out, kgrad_out, vgrad_out, gain_out, state_out,
    q, k, v, u, gain_ref, state_ref, qt, att, dfull, dlow, kpart, vpart,
    local1, before, mate1, sums1, got1, part1, back1, share1,
    local2, after, mate2, sums2, got2, part2, back2, share2,
    stats, totals, gains, gains_got,
    in_sem, send_sem, recv_sem, scan_send, scan_recv,
):
    n_seq = lax.axis_size("seq")
    n_head = lax.axis_size("head")
    me = lax.axis_index("seq")
    mine = lax.axis_index("head")
    plane = lax.rem(me, PLANES)
    line = me // PLANES
    tokens = q.shape[0]
    heads = q.shape[1] // HEAD
    half = tokens // 2

    loads = [
        pltpu.make_async_copy(src, dst, in_sem.at[i])
        for i, (src, dst) in enumerate(
            (
                (k_in, k), (v_in, v), (q_in, q),
                (u_in, u), (gain_in, gain_ref), (state_in, state_ref),
            )
        )
    ]
    for load in loads:
        load.start()

    def step_z(j):
        far = (j + 1) // 2
        away = PLANES // 2 + jnp.where(lax.rem(j, 2) == 1, -far, far)
        return lax.rem(plane + away, PLANES)

    pair, side = plane // 2, lax.rem(plane, 2)
    pairs = PLANES // 2
    mate = line * PLANES + 2 * pair + 1 - side
    away = [pairs // 2]
    for far in range(1, pairs // 2 + 1):
        away += [pairs // 2 - far, pairs // 2 + far]
    away = away[:pairs]

    def pair_at(offset):
        return lax.rem(pair + offset, pairs)

    def line_at(offset):
        return lax.rem(line + offset, LINES)

    def device(y, p, at_side):
        return y * PLANES + 2 * p + at_side

    barrier = pltpu.get_barrier_semaphore()
    for offset in away:
        for dy in (2, 1, 3, 0):
            if offset or dy:
                pl.semaphore_signal(
                    barrier, inc=1, device_id_type=MESH,
                    device_id={"seq": device(line_at(dy), pair_at(offset), side)},
                )
        pl.semaphore_signal(
            barrier, inc=1, device_id_type=MESH,
            device_id={"seq": device(line, pair_at(offset), 1 - side)},
        )
    for i in range(1, n_head):
        pl.semaphore_signal(
            barrier, inc=1, device_id={"head": lax.rem(mine + i, n_head)}, device_id_type=MESH
        )

    def cols(h):
        return slice(h * HEAD, (h + 1) * HEAD)

    def lower(x):
        r = lax.broadcasted_iota(jnp.int32, x.shape, 0)
        c = lax.broadcasted_iota(jnp.int32, x.shape, 1)
        return r >= c

    def upper(x):
        r = lax.broadcasted_iota(jnp.int32, x.shape, 0)
        c = lax.broadcasted_iota(jnp.int32, x.shape, 1)
        return r <= c

    lo, hi = slice(0, half), slice(half, tokens)

    def causal(a, b, c):
        s = nt(a[lo], b[lo])
        top = nn(jnp.where(lower(s), s, 0.0).astype(BF16), c[lo])
        s = nt(a[hi], b[hi])
        low = nn(jnp.where(lower(s), s, 0.0).astype(BF16), c[hi])
        low = low + nn(nt(a[hi], b[lo]).astype(BF16), c[lo])
        return top, low

    def anticausal(a, b, c):
        s = nt(a[hi], b[hi])
        low = nn(jnp.where(upper(s), s, 0.0).astype(BF16), c[hi])
        s = nt(a[lo], b[lo])
        top = nn(jnp.where(upper(s), s, 0.0).astype(BF16), c[lo])
        top = top + nn(nt(a[lo], b[hi]).astype(BF16), c[hi])
        return top, low

    def put_state(ref, h, value):
        first = LINES * (h % 2)
        ref[h // 2, first : first + LINES] = value.reshape(LINES, LINES, ROWS, HEAD)

    def state_of(ref, h):
        first = LINES * (h % 2)
        return ref[h // 2, first : first + LINES].reshape(HEAD, HEAD)

    loads[0].wait()
    loads[1].wait()
    for h in range(heads):
        kv = tn(k[:, cols(h)], v[:, cols(h)])
        put_state(local1, h, kv)
    for load in loads[2:]:
        load.wait()

    def forward_inside(h):
        top, low = causal(q[:, cols(h)], k[:, cols(h)], v[:, cols(h)])
        att[lo, cols(h)] = top
        att[hi, cols(h)] = low

    forward_inside(0)
    pl.semaphore_wait(barrier, n_seq // 2 - 1 + pairs + n_head - 1)

    class Scan:
        def __init__(self, local, result, other, sums, got, part, back, share, index, reverse):
            self.local, self.result, self.other, self.sums = local, result, other, sums
            self.got, self.part, self.back, self.share = got, part, back, share
            self.index, self.reverse = index, reverse

        def copy(self, src, dst, send, recv, to):
            return copy_to(
                src, dst, scan_send.at[4 * self.index + send],
                scan_recv.at[(2 * pairs + 2) * self.index + recv], seq=to,
            )

        def to_mate(self):
            for j, offset in enumerate(away):
                p = pair_at(offset)
                self.copy(self.local.at[1 - side, p], self.other.at[p], 0, j, mate).start()

        def to_owners(self):
            place = line * pairs + pair
            for j, offset in enumerate(away):
                p = pair_at(offset)
                chunk = self.other.at[p]
                self.copy(chunk, chunk, 0, j, mate).wait_recv()
                self.sums[p] = self.other[p] + self.local[side, p]
                for dy in (2, 1, 3, 0):
                    y = line_at(dy)
                    if offset or dy:
                        self.copy(
                            self.sums.at[p, y], self.got.at[place], 1, pairs, device(y, p, side)
                        ).start()
                    else:
                        self.got[place] = self.sums[p, y]

        def add_up(self, total):
            most = self.got.at[pl.ds(0, LINES * pairs - 1)]
            self.copy(most, most, 1, pairs, mate).wait_recv()
            order = range(LINES * pairs)
            for b in reversed(order) if self.reverse else order:
                self.part[b] = total
                total = total + self.got[b]
            return total

        def to_blocks(self):
            for offset in away:
                p = pair_at(offset)
                recv = pairs + 1 + (pairs - offset) % pairs
                for dy in (2, 1, 3, 0):
                    y = line_at(dy)
                    part = self.part.at[y * pairs + p]
                    if offset or dy:
                        self.copy(
                            part, self.back.at[pair, line], 2, recv, device(y, p, side)
                        ).start()
                    else:
                        self.back[pair, line] = self.part[y * pairs + p]

        def to_mate_back(self):
            second = side == (0 if self.reverse else 1)
            for offset in away:
                p = pair_at(offset)
                chunk = self.back.at[p] if offset else self.back.at[p, pl.ds(0, LINES - 1)]
                self.copy(chunk, chunk, 2, pairs + 1 + offset, mate).wait_recv()
                base = self.back[p]
                self.share[p] = base + jnp.where(second, 0.0, self.local[side, p])
                self.copy(
                    self.share.at[p], self.result.at[side, p], 3, 2 * pairs + 1, mate
                ).start()
                self.result[side, p] = base + jnp.where(second, self.other[p], 0.0)

        def finish(self):
            whole = self.result.at[0]
            self.copy(whole, whole, 3, 2 * pairs + 1, mate).wait_recv()

        def sent(self):
            whole = self.result.at[0]
            most = self.got.at[pl.ds(0, LINES * pairs - 1)]
            for send, ref in enumerate((whole, most, most, whole)):
                self.copy(ref, ref, send, 0, mate).wait_send()

    scan1 = Scan(local1, before, mate1, sums1, got1, part1, back1, share1, 0, False)
    scan2 = Scan(local2, after, mate2, sums2, got2, part2, back2, share2, 1, True)

    scan1.to_mate()
    forward_inside(1)
    scan1.to_owners()
    for h in range(heads):
        qt[h] = q[:, cols(h)].T
    forward_inside(2)
    scan1.add_up(state_ref[side * (n_seq // 2) + pair * LINES + line])
    scan1.to_blocks()
    forward_inside(3)
    scan1.to_mate_back()
    scan1.finish()

    def gain_of(h):
        return gain_ref[h : h + 1, :]

    squares = jnp.zeros((tokens, HEAD), F32)
    products = jnp.zeros((tokens, HEAD), F32)
    for h in range(heads):
        high, low = halves(state_of(before, h))
        qh = q[:, cols(h)]
        a = att[:, cols(h)] + (nn(qh, high) + nn(qh, low))
        att[:, cols(h)] = a
        squares = squares + a * a
        products = products + a * (u[:, cols(h)].astype(F32) * gain_of(h))
    blocks = tokens // HEAD
    for j in range(blocks):
        rows_j = slice(j * HEAD, (j + 1) * HEAD)
        stats[mine, j : j + 1, :] = jnp.sum(squares[rows_j].T, axis=0, keepdims=True)
        stats[mine, blocks + j : blocks + j + 1, :] = jnp.sum(
            products[rows_j].T, axis=0, keepdims=True
        )
    for i in range(1, n_head):
        copy_to(
            stats.at[mine], stats.at[mine], send_sem.at[2], recv_sem.at[2],
            head=lax.rem(mine + i, n_head),
        ).start()
    others = stats.at[pl.ds(0, n_head - 1)]
    copy_to(others, others, send_sem.at[2], recv_sem.at[2], head=mine).wait_recv()
    total = stats[0]
    for i in range(1, n_head):
        total = total + stats[i]
    mean = total * (1.0 / (heads * HEAD * n_head))
    inverse = lax.rsqrt(mean[:blocks] + 1e-06)
    coef = mean[blocks:] * inverse * inverse

    def column(x, j):
        return jnp.broadcast_to(x[j : j + 1, :], (HEAD, HEAD)).T

    inverse = jnp.concatenate([column(inverse, j) for j in range(blocks)], axis=0)
    coef = jnp.concatenate([column(coef, j) for j in range(blocks)], axis=0)
    for h in range(heads):
        scaled = u[:, cols(h)].astype(F32) * gain_of(h)
        d = inverse * (scaled - att[:, cols(h)] * coef)
        d_low = d.astype(BF16)
        dfull[:, cols(h)] = d
        dlow[:, cols(h)] = d_low
        put_state(local2, h, nn(qt[h], d_low))
    scan2.to_mate()

    gains[0] = jnp.zeros((ROWS, HEAD), F32)
    for h in range(heads):
        normed = att[:, cols(h)] * inverse
        normed_out[:, cols(h)] = (normed * gain_of(h)).astype(BF16)
        gains[0, h : h + 1, :] = jnp.sum(
            u[:, cols(h)].astype(F32) * normed, axis=0, keepdims=True
        )

    scan2.to_owners()

    def partner(i):
        step = (1, 2, 4, 8, 1, 2)[i]
        near = plane if i < 4 else line
        other = near + step - 2 * step * lax.rem(near // step, 2)
        return line * PLANES + other if i < 4 else other * PLANES + plane

    def gain_copy(i):
        return copy_to(
            gains.at[i], gains_got.at[i], send_sem.at[7 + i], recv_sem.at[7 + i], seq=partner(i)
        )

    def gain_step(i):
        gain_copy(i).wait_recv()
        gains[i + 1] = gains[i] + gains_got[i]
        if i < 5:
            gain_copy(i + 1).start()

    gain_copy(0).start()

    def query_gradient(h):
        d_low = dlow[:, cols(h)]
        d_rest = (dfull[:, cols(h)] - d_low.astype(F32)).astype(BF16)
        high, low = halves(state_of(before, h))
        carried = nt(d_low, high) + (nt(d_low, low) + nt(d_rest, high))
        top, low = causal(d_low, v[:, cols(h)], k[:, cols(h)])
        qgrad_out[lo, cols(h)] = (top + carried[lo]).astype(BF16)
        qgrad_out[hi, cols(h)] = (low + carried[hi]).astype(BF16)

    for h in range(heads):
        query_gradient(h)
        if h == 1:
            gain_step(0)
    gain_step(1)

    totals[me] = scan2.add_up(jnp.zeros((ROWS, HEAD), F32))

    def send_total(j, carry):
        copy_to(
            totals.at[me], totals.at[me], send_sem.at[5], recv_sem.at[5],
            seq=line * PLANES + step_z(j),
        ).start()
        return carry

    lax.fori_loop(0, PLANES - 1, send_total, 0)
    scan2.to_blocks()

    for h in range(heads):
        top, low = anticausal(v[:, cols(h)], dlow[:, cols(h)], q[:, cols(h)])
        kpart[lo, cols(h)] = top
        kpart[hi, cols(h)] = low
        top, low = anticausal(k[:, cols(h)], q[:, cols(h)], dlow[:, cols(h)])
        vpart[lo, cols(h)] = top
        vpart[hi, cols(h)] = low

    scan2.to_mate_back()
    row = totals.at[pl.ds(line * PLANES, PLANES)]
    some = totals.at[pl.ds(0, PLANES - 1)]
    copy_to(some, some, send_sem.at[5], recv_sem.at[5], seq=me).wait_recv()
    for i in (2, 1, 3):
        copy_to(
            row, row, send_sem.at[6], recv_sem.at[6],
            seq=lax.rem(line + i, LINES) * PLANES + plane,
        ).start()
    gain_step(2)

    scan2.finish()
    for h in range(heads):
        high, low = halves(state_of(after, h))
        vh, kh = v[:, cols(h)], k[:, cols(h)]
        kgrad_out[:, cols(h)] = (kpart[:, cols(h)] + (nt(vh, high) + nt(vh, low))).astype(BF16)
        vgrad_out[:, cols(h)] = (vpart[:, cols(h)] + (nn(kh, high) + nn(kh, low))).astype(BF16)

    gain_step(3)
    three = totals.at[pl.ds(0, (LINES - 1) * PLANES)]
    copy_to(three, three, send_sem.at[6], recv_sem.at[6], seq=me).wait_recv()
    for at in range(n_seq):
        owner = device(at % LINES, at % (n_seq // 2) // LINES, at // (n_seq // 2))
        state_out[at] = totals[owner]
    gain_step(4)
    gain_step(5)
    gain_out[...] = gains[6, :heads, :]

    scan1.sent()
    scan2.sent()
    copy_to(others, others, send_sem.at[2], recv_sem.at[2], head=mine).wait_send()
    copy_to(some, some, send_sem.at[5], recv_sem.at[5], seq=me).wait_send()
    copy_to(three, three, send_sem.at[6], recv_sem.at[6], seq=me).wait_send()
    for i in range(6):
        gain_copy(i).wait_send()


def store_kernel(*refs):
    n = len(refs) // 2
    stores = [pltpu.make_async_copy(refs[i], refs[n + i], refs[-1].at[i]) for i in range(n)]
    for store in stores:
        store.start()
    for store in stores:
        store.wait()


def per_device(query_in, key_in, value_in, upstream, norm_gain, state_in):
    tokens, columns = query_in.shape
    heads = state_in.shape[0]
    n_seq = lax.axis_size("seq")
    n_head = lax.axis_size("head")
    wide = jax.ShapeDtypeStruct((tokens, columns), BF16)
    slices = (n_seq, ROWS, HEAD)
    vmem = pl.BlockSpec(memory_space=pltpu.VMEM)
    anywhere = pl.BlockSpec(memory_space=pl.ANY)
    hbm = pl.BlockSpec(memory_space=pltpu.HBM)
    low = pltpu.VMEM((tokens, columns), BF16)
    full = pltpu.VMEM((tokens, columns), F32)
    pairs = PLANES // 2
    whole = pltpu.VMEM((2, pairs, LINES, ROWS, HEAD), F32)
    half = pltpu.VMEM((pairs, LINES, ROWS, HEAD), F32)
    flat = pltpu.VMEM((pairs * LINES, ROWS, HEAD), F32)
    shapes = (
        wide, wide, wide, wide,
        jax.ShapeDtypeStruct((heads, HEAD), F32),
        jax.ShapeDtypeStruct(slices, F32),
    )
    outs = pl.pallas_call(
        kernel,
        name="attention_and_gradients",
        out_shape=shapes,
        in_specs=[hbm] * 6,
        out_specs=[vmem] * 6,
        scratch_shapes=[low] * 4
        + [pltpu.VMEM((heads, HEAD), F32), pltpu.VMEM(slices, F32)]
        + [pltpu.VMEM((heads, HEAD, tokens), BF16), full, full, low, full, full]
        + ([whole] * 2 + [half] * 2 + [flat] * 2 + [half] * 2) * 2
        + [
            pltpu.VMEM((n_head, ROWS, HEAD), F32),
            pltpu.VMEM(slices, F32),
            pltpu.VMEM((7, ROWS, HEAD), F32),
            pltpu.VMEM((6, ROWS, HEAD), F32),
            pltpu.SemaphoreType.DMA((6,)),
            pltpu.SemaphoreType.DMA((13,)),
            pltpu.SemaphoreType.DMA((13,)),
            pltpu.SemaphoreType.DMA((8,)),
            pltpu.SemaphoreType.DMA((2 * (2 * pairs + 2),)),
        ],
        compiler_params=pltpu.CompilerParams(
            collective_id=0, has_side_effects=True, vmem_limit_bytes=51 << 20
        ),
    )(
        query_in, key_in, value_in, upstream,
        norm_gain.reshape(heads, HEAD), state_in.reshape(slices),
    )
    outs = pl.pallas_call(
        store_kernel,
        name="store",
        out_shape=shapes,
        in_specs=[anywhere] * 6,
        out_specs=[hbm] * 6,
        scratch_shapes=[pltpu.SemaphoreType.DMA((6,))],
        compiler_params=pltpu.CompilerParams(vmem_limit_bytes=1 << 20),
    )(*outs)
    return (
        outs[0], outs[1], outs[2], outs[3],
        outs[4].reshape(heads * HEAD), outs[5].reshape(state_in.shape),
    )


def solution(mesh):
    wide = P("seq", "head")
    return jax.shard_map(
        per_device,
        mesh=mesh,
        in_specs=(wide, wide, wide, wide, P("head"), P("head", None, None)),
        out_specs=(wide, wide, wide, wide, P("head"), P("head", None, None)),
        check_vma=False,
    )
```

```python
import functools

import jax
import jax.numpy as jnp
from jax import lax
from jax.experimental import pallas as pl
from jax.experimental.pallas import tpu as pltpu
from jax.sharding import PartitionSpec as P

F32 = jnp.float32
BF16 = jnp.bfloat16
MESH = pl.DeviceIdType.MESH
HEAD = 128
ROWS = 8
PLANES = 16
LINES = 4


def nn(a, b):
    return lax.dot_general(a, b, (((1,), (0,)), ((), ())), preferred_element_type=F32)


def nt(a, b):
    return lax.dot_general(a, b, (((1,), (1,)), ((), ())), preferred_element_type=F32)


def tn(a, b):
    return lax.dot_general(a, b, (((0,), (0,)), ((), ())), preferred_element_type=F32)


def halves(x):
    high = x.astype(BF16)
    return high, (x - high.astype(F32)).astype(BF16)


def copy_to(src, dst, send, recv, **where):
    return pltpu.make_async_remote_copy(
        src, dst, send, recv, device_id=where, device_id_type=MESH
    )


def kernel(
    q_in, k_in, v_in, u_in, gain_in, state_in,
    normed_out, qgrad_out, kgrad_out, vgrad_out, gain_out, state_out,
    q, k, v, u, gain_ref, state_ref, qt, att, dfull, dlow, kpart, vpart,
    local1, before, mate1, sums1, got1, part1, back1, share1,
    local2, after, mate2, sums2, got2, part2, back2, share2,
    stats, totals, gains, line_gains, all_gains,
    in_sem, send_sem, recv_sem, scan_send, scan_recv,
):
    n_seq = lax.axis_size("seq")
    n_head = lax.axis_size("head")
    me = lax.axis_index("seq")
    mine = lax.axis_index("head")
    plane = lax.rem(me, PLANES)
    line = me // PLANES
    tokens = q.shape[0]
    heads = q.shape[1] // HEAD
    half = tokens // 2

    loads = [
        pltpu.make_async_copy(src, dst, in_sem.at[i])
        for i, (src, dst) in enumerate(
            (
                (k_in, k), (v_in, v), (q_in, q),
                (u_in, u), (gain_in, gain_ref), (state_in, state_ref),
            )
        )
    ]
    for load in loads:
        load.start()

    def step_z(j):
        far = (j + 1) // 2
        away = PLANES // 2 + jnp.where(lax.rem(j, 2) == 1, -far, far)
        return lax.rem(plane + away, PLANES)

    pair, side = plane // 2, lax.rem(plane, 2)
    pairs = PLANES // 2
    mate = line * PLANES + 2 * pair + 1 - side
    away = [pairs // 2]
    for far in range(1, pairs // 2 + 1):
        away += [pairs // 2 - far, pairs // 2 + far]
    away = away[:pairs]

    def pair_at(offset):
        return lax.rem(pair + offset, pairs)

    def line_at(offset):
        return lax.rem(line + offset, LINES)

    def device(y, p, at_side):
        return y * PLANES + 2 * p + at_side

    barrier = pltpu.get_barrier_semaphore()
    for offset in away:
        for dy in (2, 1, 3, 0):
            if offset or dy:
                pl.semaphore_signal(
                    barrier, inc=1, device_id_type=MESH,
                    device_id={"seq": device(line_at(dy), pair_at(offset), side)},
                )
        pl.semaphore_signal(
            barrier, inc=1, device_id_type=MESH,
            device_id={"seq": device(line, pair_at(offset), 1 - side)},
        )
    for i in range(1, n_head):
        pl.semaphore_signal(
            barrier, inc=1, device_id={"head": lax.rem(mine + i, n_head)}, device_id_type=MESH
        )

    def cols(h):
        return slice(h * HEAD, (h + 1) * HEAD)

    def lower(x):
        r = lax.broadcasted_iota(jnp.int32, x.shape, 0)
        c = lax.broadcasted_iota(jnp.int32, x.shape, 1)
        return r >= c

    def upper(x):
        r = lax.broadcasted_iota(jnp.int32, x.shape, 0)
        c = lax.broadcasted_iota(jnp.int32, x.shape, 1)
        return r <= c

    lo, hi = slice(0, half), slice(half, tokens)

    def causal(a, b, c):
        s = nt(a[lo], b[lo])
        top = nn(jnp.where(lower(s), s, 0.0).astype(BF16), c[lo])
        s = nt(a[hi], b[hi])
        low = nn(jnp.where(lower(s), s, 0.0).astype(BF16), c[hi])
        low = low + nn(nt(a[hi], b[lo]).astype(BF16), c[lo])
        return top, low

    def anticausal(a, b, c):
        s = nt(a[hi], b[hi])
        low = nn(jnp.where(upper(s), s, 0.0).astype(BF16), c[hi])
        s = nt(a[lo], b[lo])
        top = nn(jnp.where(upper(s), s, 0.0).astype(BF16), c[lo])
        top = top + nn(nt(a[lo], b[hi]).astype(BF16), c[hi])
        return top, low

    def put_state(ref, h, value):
        first = LINES * (h % 2)
        ref[h // 2, first : first + LINES] = value.reshape(LINES, LINES, ROWS, HEAD)

    def state_of(ref, h):
        first = LINES * (h % 2)
        return ref[h // 2, first : first + LINES].reshape(HEAD, HEAD)

    loads[0].wait()
    loads[1].wait()
    for h in range(heads):
        kv = tn(k[:, cols(h)], v[:, cols(h)])
        put_state(local1, h, kv)
    for load in loads[2:]:
        load.wait()

    def forward_inside(h):
        top, low = causal(q[:, cols(h)], k[:, cols(h)], v[:, cols(h)])
        att[lo, cols(h)] = top
        att[hi, cols(h)] = low

    forward_inside(0)
    pl.semaphore_wait(barrier, n_seq // 2 - 1 + pairs + n_head - 1)

    class Scan:
        def __init__(self, local, result, other, sums, got, part, back, share, index, reverse):
            self.local, self.result, self.other, self.sums = local, result, other, sums
            self.got, self.part, self.back, self.share = got, part, back, share
            self.index, self.reverse = index, reverse

        def copy(self, src, dst, send, recv, to):
            return copy_to(
                src, dst, scan_send.at[4 * self.index + send],
                scan_recv.at[(2 * pairs + 2) * self.index + recv], seq=to,
            )

        def to_mate(self):
            for j, offset in enumerate(away):
                p = pair_at(offset)
                self.copy(self.local.at[1 - side, p], self.other.at[p], 0, j, mate).start()

        def to_owners(self):
            place = line * pairs + pair
            for j, offset in enumerate(away):
                p = pair_at(offset)
                chunk = self.other.at[p]
                self.copy(chunk, chunk, 0, j, mate).wait_recv()
                self.sums[p] = self.other[p] + self.local[side, p]
                for dy in (2, 1, 3, 0):
                    y = line_at(dy)
                    if offset or dy:
                        self.copy(
                            self.sums.at[p, y], self.got.at[place], 1, pairs, device(y, p, side)
                        ).start()
                    else:
                        self.got[place] = self.sums[p, y]

        def add_up(self, total):
            most = self.got.at[pl.ds(0, LINES * pairs - 1)]
            self.copy(most, most, 1, pairs, mate).wait_recv()
            order = range(LINES * pairs)
            for b in reversed(order) if self.reverse else order:
                self.part[b] = total
                total = total + self.got[b]
            return total

        def to_blocks(self):
            for offset in away:
                p = pair_at(offset)
                recv = pairs + 1 + (pairs - offset) % pairs
                for dy in (2, 1, 3, 0):
                    y = line_at(dy)
                    part = self.part.at[y * pairs + p]
                    if offset or dy:
                        self.copy(
                            part, self.back.at[pair, line], 2, recv, device(y, p, side)
                        ).start()
                    else:
                        self.back[pair, line] = self.part[y * pairs + p]

        def to_mate_back(self):
            second = side == (0 if self.reverse else 1)
            for offset in away:
                p = pair_at(offset)
                chunk = self.back.at[p] if offset else self.back.at[p, pl.ds(0, LINES - 1)]
                self.copy(chunk, chunk, 2, pairs + 1 + offset, mate).wait_recv()
                base = self.back[p]
                self.share[p] = base + jnp.where(second, 0.0, self.local[side, p])
                self.copy(
                    self.share.at[p], self.result.at[side, p], 3, 2 * pairs + 1, mate
                ).start()
                self.result[side, p] = base + jnp.where(second, self.other[p], 0.0)

        def finish(self):
            whole = self.result.at[0]
            self.copy(whole, whole, 3, 2 * pairs + 1, mate).wait_recv()

        def sent(self):
            whole = self.result.at[0]
            most = self.got.at[pl.ds(0, LINES * pairs - 1)]
            for send, ref in enumerate((whole, most, most, whole)):
                self.copy(ref, ref, send, 0, mate).wait_send()

    scan1 = Scan(local1, before, mate1, sums1, got1, part1, back1, share1, 0, False)
    scan2 = Scan(local2, after, mate2, sums2, got2, part2, back2, share2, 1, True)

    scan1.to_mate()
    forward_inside(1)
    scan1.to_owners()
    for h in range(heads):
        qt[h] = q[:, cols(h)].T
    forward_inside(2)
    scan1.add_up(state_ref[side * (n_seq // 2) + pair * LINES + line])
    scan1.to_blocks()
    forward_inside(3)
    scan1.to_mate_back()
    scan1.finish()

    def gain_of(h):
        return gain_ref[h : h + 1, :]

    squares = jnp.zeros((tokens, HEAD), F32)
    products = jnp.zeros((tokens, HEAD), F32)
    for h in range(heads):
        high, low = halves(state_of(before, h))
        qh = q[:, cols(h)]
        a = att[:, cols(h)] + (nn(qh, high) + nn(qh, low))
        att[:, cols(h)] = a
        squares = squares + a * a
        products = products + a * (u[:, cols(h)].astype(F32) * gain_of(h))
    blocks = tokens // HEAD
    for j in range(blocks):
        rows_j = slice(j * HEAD, (j + 1) * HEAD)
        stats[mine, j : j + 1, :] = jnp.sum(squares[rows_j].T, axis=0, keepdims=True)
        stats[mine, blocks + j : blocks + j + 1, :] = jnp.sum(
            products[rows_j].T, axis=0, keepdims=True
        )
    for i in range(1, n_head):
        copy_to(
            stats.at[mine], stats.at[mine], send_sem.at[2], recv_sem.at[2],
            head=lax.rem(mine + i, n_head),
        ).start()
    others = stats.at[pl.ds(0, n_head - 1)]
    copy_to(others, others, send_sem.at[2], recv_sem.at[2], head=mine).wait_recv()
    total = stats[0]
    for i in range(1, n_head):
        total = total + stats[i]
    mean = total * (1.0 / (heads * HEAD * n_head))
    inverse = lax.rsqrt(mean[:blocks] + 1e-06)
    coef = mean[blocks:] * inverse * inverse

    def column(x, j):
        return jnp.broadcast_to(x[j : j + 1, :], (HEAD, HEAD)).T

    inverse = jnp.concatenate([column(inverse, j) for j in range(blocks)], axis=0)
    coef = jnp.concatenate([column(coef, j) for j in range(blocks)], axis=0)
    for h in range(heads):
        scaled = u[:, cols(h)].astype(F32) * gain_of(h)
        d = inverse * (scaled - att[:, cols(h)] * coef)
        d_low = d.astype(BF16)
        dfull[:, cols(h)] = d
        dlow[:, cols(h)] = d_low
        put_state(local2, h, nn(qt[h], d_low))
    scan2.to_mate()

    gains[0] = jnp.zeros((ROWS, HEAD), F32)
    for h in range(heads):
        normed = att[:, cols(h)] * inverse
        normed_out[:, cols(h)] = (normed * gain_of(h)).astype(BF16)
        gains[0, h : h + 1, :] = jnp.sum(
            u[:, cols(h)].astype(F32) * normed, axis=0, keepdims=True
        )

    to_mate = copy_to(gains.at[0], gains.at[3], send_sem.at[7], recv_sem.at[7], seq=mate)
    to_mate.start()
    scan2.to_owners()

    to_mate.wait_recv()
    gains[1] = gains[0] + gains[3]
    line_gains[pair] = gains[1]
    for offset in away[:-1]:
        copy_to(
            gains.at[1], line_gains.at[pair], send_sem.at[8], recv_sem.at[8],
            seq=device(line, pair_at(offset), side),
        ).start()

    def query_gradient(h):
        d_low = dlow[:, cols(h)]
        d_rest = (dfull[:, cols(h)] - d_low.astype(F32)).astype(BF16)
        high, low = halves(state_of(before, h))
        carried = nt(d_low, high) + (nt(d_low, low) + nt(d_rest, high))
        top, low = causal(d_low, v[:, cols(h)], k[:, cols(h)])
        qgrad_out[lo, cols(h)] = (top + carried[lo]).astype(BF16)
        qgrad_out[hi, cols(h)] = (low + carried[hi]).astype(BF16)

    for h in range(heads):
        query_gradient(h)

    totals[me] = scan2.add_up(jnp.zeros((ROWS, HEAD), F32))

    def send_total(j, carry):
        copy_to(
            totals.at[me], totals.at[me], send_sem.at[5], recv_sem.at[5],
            seq=line * PLANES + step_z(j),
        ).start()
        return carry

    lax.fori_loop(0, PLANES - 1, send_total, 0)
    scan2.to_blocks()

    for h in range(heads):
        top, low = anticausal(v[:, cols(h)], dlow[:, cols(h)], q[:, cols(h)])
        kpart[lo, cols(h)] = top
        kpart[hi, cols(h)] = low
        top, low = anticausal(k[:, cols(h)], q[:, cols(h)], dlow[:, cols(h)])
        vpart[lo, cols(h)] = top
        vpart[hi, cols(h)] = low

    some = totals.at[pl.ds(0, PLANES - 1)]
    copy_to(some, some, send_sem.at[5], recv_sem.at[5], seq=me).wait_recv()
    row = totals.at[pl.ds(line * PLANES, PLANES)]
    for i in (2, 1, 3):
        copy_to(
            row, row, send_sem.at[6], recv_sem.at[6], seq=device(line_at(i), pair, side)
        ).start()
    seven = line_gains.at[pl.ds(0, pairs - 1)]
    copy_to(seven, seven, send_sem.at[8], recv_sem.at[8], seq=me).wait_recv()
    gain = line_gains[0]
    for i in range(1, pairs):
        gain = gain + line_gains[i]
    gains[2] = gain
    all_gains[line] = gain
    for i in (2, 1, 3):
        copy_to(
            gains.at[2], all_gains.at[line], send_sem.at[9], recv_sem.at[9],
            seq=device(line_at(i), pair, side),
        ).start()

    def other_gradients(part):
        for i in range(heads // 2):
            at = pl.ds(pl.multiple_of((heads // 2 * part + i) * HEAD, HEAD), HEAD)
            rows_i = after[part, LINES * i : LINES * (i + 1)].reshape(HEAD, HEAD)
            high, low = halves(rows_i)
            vh, kh = v[:, at], k[:, at]
            kgrad_out[:, at] = (kpart[:, at] + (nt(vh, high) + nt(vh, low))).astype(BF16)
            vgrad_out[:, at] = (vpart[:, at] + (nn(kh, high) + nn(kh, low))).astype(BF16)

    scan2.to_mate_back()
    other_gradients(side)
    scan2.finish()
    other_gradients(1 - side)

    three = totals.at[pl.ds(0, (LINES - 1) * PLANES)]
    copy_to(three, three, send_sem.at[6], recv_sem.at[6], seq=me).wait_recv()
    for at in range(n_seq):
        owner = device(at % LINES, at % (n_seq // 2) // LINES, at // (n_seq // 2))
        state_out[at] = totals[owner]
    some_gains = all_gains.at[pl.ds(0, LINES - 1)]
    copy_to(some_gains, some_gains, send_sem.at[9], recv_sem.at[9], seq=me).wait_recv()
    gain = all_gains[0]
    for i in range(1, LINES):
        gain = gain + all_gains[i]
    gain_out[...] = gain[:heads]

    scan1.sent()
    scan2.sent()
    copy_to(others, others, send_sem.at[2], recv_sem.at[2], head=mine).wait_send()
    copy_to(some, some, send_sem.at[5], recv_sem.at[5], seq=me).wait_send()
    copy_to(three, three, send_sem.at[6], recv_sem.at[6], seq=me).wait_send()
    to_mate.wait_send()
    copy_to(seven, seven, send_sem.at[8], recv_sem.at[8], seq=me).wait_send()
    copy_to(some_gains, some_gains, send_sem.at[9], recv_sem.at[9], seq=me).wait_send()


def store_kernel(*refs):
    n = len(refs) // 2
    stores = [pltpu.make_async_copy(refs[i], refs[n + i], refs[-1].at[i]) for i in range(n)]
    for store in stores:
        store.start()
    for store in stores:
        store.wait()


def per_device(query_in, key_in, value_in, upstream, norm_gain, state_in):
    tokens, columns = query_in.shape
    heads = state_in.shape[0]
    n_seq = lax.axis_size("seq")
    n_head = lax.axis_size("head")
    wide = jax.ShapeDtypeStruct((tokens, columns), BF16)
    slices = (n_seq, ROWS, HEAD)
    vmem = pl.BlockSpec(memory_space=pltpu.VMEM)
    anywhere = pl.BlockSpec(memory_space=pl.ANY)
    hbm = pl.BlockSpec(memory_space=pltpu.HBM)
    low = pltpu.VMEM((tokens, columns), BF16)
    full = pltpu.VMEM((tokens, columns), F32)
    pairs = PLANES // 2
    whole = pltpu.VMEM((2, pairs, LINES, ROWS, HEAD), F32)
    half = pltpu.VMEM((pairs, LINES, ROWS, HEAD), F32)
    flat = pltpu.VMEM((pairs * LINES, ROWS, HEAD), F32)
    shapes = (
        wide, wide, wide, wide,
        jax.ShapeDtypeStruct((heads, HEAD), F32),
        jax.ShapeDtypeStruct(slices, F32),
    )
    outs = pl.pallas_call(
        kernel,
        name="attention_and_gradients",
        out_shape=shapes,
        in_specs=[hbm] * 6,
        out_specs=[vmem] * 6,
        scratch_shapes=[low] * 4
        + [pltpu.VMEM((heads, HEAD), F32), pltpu.VMEM(slices, F32)]
        + [pltpu.VMEM((heads, HEAD, tokens), BF16), full, full, low, full, full]
        + ([whole] * 2 + [half] * 2 + [flat] * 2 + [half] * 2) * 2
        + [
            pltpu.VMEM((n_head, ROWS, HEAD), F32),
            pltpu.VMEM(slices, F32),
            pltpu.VMEM((4, ROWS, HEAD), F32),
            pltpu.VMEM((pairs, ROWS, HEAD), F32),
            pltpu.VMEM((LINES, ROWS, HEAD), F32),
            pltpu.SemaphoreType.DMA((6,)),
            pltpu.SemaphoreType.DMA((10,)),
            pltpu.SemaphoreType.DMA((10,)),
            pltpu.SemaphoreType.DMA((8,)),
            pltpu.SemaphoreType.DMA((2 * (2 * pairs + 2),)),
        ],
        compiler_params=pltpu.CompilerParams(
            collective_id=0, has_side_effects=True, vmem_limit_bytes=51 << 20
        ),
    )(
        query_in, key_in, value_in, upstream,
        norm_gain.reshape(heads, HEAD), state_in.reshape(slices),
    )
    outs = pl.pallas_call(
        store_kernel,
        name="store",
        out_shape=shapes,
        in_specs=[anywhere] * 6,
        out_specs=[hbm] * 6,
        scratch_shapes=[pltpu.SemaphoreType.DMA((6,))],
        compiler_params=pltpu.CompilerParams(vmem_limit_bytes=1 << 20),
    )(*outs)
    return (
        outs[0], outs[1], outs[2], outs[3],
        outs[4].reshape(heads * HEAD), outs[5].reshape(state_in.shape),
    )


def solution(mesh):
    wide = P("seq", "head")
    return jax.shard_map(
        per_device,
        mesh=mesh,
        in_specs=(wide, wide, wide, wide, P("head"), P("head", None, None)),
        out_specs=(wide, wide, wide, wide, P("head"), P("head", None, None)),
        check_vma=False,
    )
```

```python
import functools

import jax
import jax.numpy as jnp
from jax import lax
from jax.experimental import pallas as pl
from jax.experimental.pallas import tpu as pltpu
from jax.sharding import PartitionSpec as P

F32 = jnp.float32
BF16 = jnp.bfloat16
MESH = pl.DeviceIdType.MESH
HEAD = 128
ROWS = 8
PLANES = 16
LINES = 4


def nn(a, b):
    return lax.dot_general(a, b, (((1,), (0,)), ((), ())), preferred_element_type=F32)


def nt(a, b):
    return lax.dot_general(a, b, (((1,), (1,)), ((), ())), preferred_element_type=F32)


def tn(a, b):
    return lax.dot_general(a, b, (((0,), (0,)), ((), ())), preferred_element_type=F32)


def halves(x):
    high = x.astype(BF16)
    return high, (x - high.astype(F32)).astype(BF16)


def copy_to(src, dst, send, recv, **where):
    return pltpu.make_async_remote_copy(
        src, dst, send, recv, device_id=where, device_id_type=MESH
    )


def kernel(
    q_in, k_in, v_in, u_in, gain_in, state_in,
    normed_out, qgrad_out, kgrad_out, vgrad_out, gain_out, state_out,
    q, k, v, u, gain_ref, state_ref, qt, att, dfull, dlow, kpart, vpart,
    local1, before, mate1, sums1, got1, part1, back1, share1,
    local2, after, mate2, sums2, got2, part2, back2, share2,
    stats, totals, gains, line_gains, all_gains,
    in_sem, send_sem, recv_sem, scan_send, scan_recv,
):
    n_seq = lax.axis_size("seq")
    n_head = lax.axis_size("head")
    me = lax.axis_index("seq")
    mine = lax.axis_index("head")
    plane = lax.rem(me, PLANES)
    line = me // PLANES
    tokens = q.shape[0]
    heads = q.shape[1] // HEAD
    half = tokens // 2

    loads = [
        pltpu.make_async_copy(src, dst, in_sem.at[i])
        for i, (src, dst) in enumerate(
            (
                (k_in, k), (v_in, v), (q_in, q),
                (u_in, u), (gain_in, gain_ref), (state_in, state_ref),
            )
        )
    ]
    for load in loads:
        load.start()

    def step_z(j):
        far = (j + 1) // 2
        away = PLANES // 2 + jnp.where(lax.rem(j, 2) == 1, -far, far)
        return lax.rem(plane + away, PLANES)

    pair, side = plane // 2, lax.rem(plane, 2)
    pairs = PLANES // 2
    mate = line * PLANES + 2 * pair + 1 - side
    away = [pairs // 2]
    for far in range(1, pairs // 2 + 1):
        away += [pairs // 2 - far, pairs // 2 + far]
    away = away[:pairs]

    def pair_at(offset):
        return lax.rem(pair + offset, pairs)

    def line_at(offset):
        return lax.rem(line + offset, LINES)

    def device(y, p, at_side):
        return y * PLANES + 2 * p + at_side

    barrier = pltpu.get_barrier_semaphore()
    for offset in away:
        for dy in (2, 1, 3, 0):
            if offset or dy:
                pl.semaphore_signal(
                    barrier, inc=1, device_id_type=MESH,
                    device_id={"seq": device(line_at(dy), pair_at(offset), side)},
                )
        pl.semaphore_signal(
            barrier, inc=1, device_id_type=MESH,
            device_id={"seq": device(line, pair_at(offset), 1 - side)},
        )
    for i in range(1, n_head):
        pl.semaphore_signal(
            barrier, inc=1, device_id={"head": lax.rem(mine + i, n_head)}, device_id_type=MESH
        )

    def cols(h):
        return slice(h * HEAD, (h + 1) * HEAD)

    def lower(x):
        r = lax.broadcasted_iota(jnp.int32, x.shape, 0)
        c = lax.broadcasted_iota(jnp.int32, x.shape, 1)
        return r >= c

    def upper(x):
        r = lax.broadcasted_iota(jnp.int32, x.shape, 0)
        c = lax.broadcasted_iota(jnp.int32, x.shape, 1)
        return r <= c

    lo, hi = slice(0, half), slice(half, tokens)

    def causal(a, b, c):
        s = nt(a[lo], b[lo])
        top = nn(jnp.where(lower(s), s, 0.0).astype(BF16), c[lo])
        s = nt(a[hi], b[hi])
        low = nn(jnp.where(lower(s), s, 0.0).astype(BF16), c[hi])
        low = low + nn(nt(a[hi], b[lo]).astype(BF16), c[lo])
        return top, low

    def anticausal(a, b, c):
        s = nt(a[hi], b[hi])
        low = nn(jnp.where(upper(s), s, 0.0).astype(BF16), c[hi])
        s = nt(a[lo], b[lo])
        top = nn(jnp.where(upper(s), s, 0.0).astype(BF16), c[lo])
        top = top + nn(nt(a[lo], b[hi]).astype(BF16), c[hi])
        return top, low

    def put_state(ref, h, value):
        first = LINES * (h % 2)
        ref[h // 2, first : first + LINES] = value.reshape(LINES, LINES, ROWS, HEAD)

    def state_of(ref, h):
        first = LINES * (h % 2)
        return ref[h // 2, first : first + LINES].reshape(HEAD, HEAD)

    loads[0].wait()
    loads[1].wait()
    for h in range(heads):
        kv = tn(k[:, cols(h)], v[:, cols(h)])
        put_state(local1, h, kv)
    for load in loads[2:]:
        load.wait()

    def forward_inside(h):
        top, low = causal(q[:, cols(h)], k[:, cols(h)], v[:, cols(h)])
        att[lo, cols(h)] = top
        att[hi, cols(h)] = low

    forward_inside(0)
    pl.semaphore_wait(barrier, n_seq // 2 - 1 + pairs + n_head - 1)

    class Scan:
        def __init__(self, local, result, other, sums, got, part, back, share, index, reverse):
            self.local, self.result, self.other, self.sums = local, result, other, sums
            self.got, self.part, self.back, self.share = got, part, back, share
            self.index, self.reverse = index, reverse

        def copy(self, src, dst, send, recv, to):
            return copy_to(
                src, dst, scan_send.at[4 * self.index + send],
                scan_recv.at[(2 * pairs + 2) * self.index + recv], seq=to,
            )

        def to_mate(self):
            for j, offset in enumerate(away):
                p = pair_at(offset)
                self.copy(self.local.at[1 - side, p], self.other.at[p], 0, j, mate).start()

        def to_owners(self):
            place = line * pairs + pair
            for j, offset in enumerate(away):
                p = pair_at(offset)
                chunk = self.other.at[p]
                self.copy(chunk, chunk, 0, j, mate).wait_recv()
                self.sums[p] = self.other[p] + self.local[side, p]
                for dy in (2, 1, 3, 0):
                    y = line_at(dy)
                    if offset or dy:
                        self.copy(
                            self.sums.at[p, y], self.got.at[place], 1, pairs, device(y, p, side)
                        ).start()
                    else:
                        self.got[place] = self.sums[p, y]

        def add_up(self, total):
            most = self.got.at[pl.ds(0, LINES * pairs - 1)]
            self.copy(most, most, 1, pairs, mate).wait_recv()
            order = range(LINES * pairs)
            for b in reversed(order) if self.reverse else order:
                self.part[b] = total
                total = total + self.got[b]
            return total

        def to_blocks(self):
            for offset in away:
                p = pair_at(offset)
                recv = pairs + 1 + (pairs - offset) % pairs
                for dy in (2, 1, 3, 0):
                    y = line_at(dy)
                    part = self.part.at[y * pairs + p]
                    if offset or dy:
                        self.copy(
                            part, self.back.at[pair, line], 2, recv, device(y, p, side)
                        ).start()
                    else:
                        self.back[pair, line] = self.part[y * pairs + p]

        def to_mate_back(self):
            second = side == (0 if self.reverse else 1)
            for offset in reversed(away):
                p = pair_at(offset)
                chunk = self.back.at[p] if offset else self.back.at[p, pl.ds(0, LINES - 1)]
                self.copy(chunk, chunk, 2, pairs + 1 + offset, mate).wait_recv()
                base = self.back[p]
                self.share[p] = base + jnp.where(second, 0.0, self.local[side, p])
                self.copy(
                    self.share.at[p], self.result.at[side, p], 3, 2 * pairs + 1, mate
                ).start()
                self.result[side, p] = base + jnp.where(second, self.other[p], 0.0)

        def finish(self):
            whole = self.result.at[0]
            self.copy(whole, whole, 3, 2 * pairs + 1, mate).wait_recv()

        def sent(self):
            whole = self.result.at[0]
            most = self.got.at[pl.ds(0, LINES * pairs - 1)]
            for send, ref in enumerate((whole, most, most, whole)):
                self.copy(ref, ref, send, 0, mate).wait_send()

    scan1 = Scan(local1, before, mate1, sums1, got1, part1, back1, share1, 0, False)
    scan2 = Scan(local2, after, mate2, sums2, got2, part2, back2, share2, 1, True)

    scan1.to_mate()
    forward_inside(1)
    scan1.to_owners()
    for h in range(heads):
        qt[h] = q[:, cols(h)].T
    forward_inside(2)
    scan1.add_up(state_ref[side * (n_seq // 2) + pair * LINES + line])
    scan1.to_blocks()
    forward_inside(3)
    scan1.to_mate_back()

    def gain_of(h):
        return gain_ref[h : h + 1, :]

    def forward_carried(part, squares, products):
        for i in range(heads // 2):
            h = heads // 2 * part + i
            at = pl.ds(pl.multiple_of(h * HEAD, HEAD), HEAD)
            high, low = halves(before[part, LINES * i : LINES * (i + 1)].reshape(HEAD, HEAD))
            a = att[:, at] + (nn(q[:, at], high) + nn(q[:, at], low))
            att[:, at] = a
            squares = squares + a * a
            products = products + a * (u[:, at].astype(F32) * gain_ref[pl.ds(h, 1), :])
        return squares, products

    nothing = jnp.zeros((tokens, HEAD), F32)
    squares, products = forward_carried(side, nothing, nothing)
    scan1.finish()
    squares, products = forward_carried(1 - side, squares, products)
    blocks = tokens // HEAD
    for j in range(blocks):
        rows_j = slice(j * HEAD, (j + 1) * HEAD)
        stats[mine, j : j + 1, :] = jnp.sum(squares[rows_j].T, axis=0, keepdims=True)
        stats[mine, blocks + j : blocks + j + 1, :] = jnp.sum(
            products[rows_j].T, axis=0, keepdims=True
        )
    for i in range(1, n_head):
        copy_to(
            stats.at[mine], stats.at[mine], send_sem.at[2], recv_sem.at[2],
            head=lax.rem(mine + i, n_head),
        ).start()
    others = stats.at[pl.ds(0, n_head - 1)]
    copy_to(others, others, send_sem.at[2], recv_sem.at[2], head=mine).wait_recv()
    total = stats[0]
    for i in range(1, n_head):
        total = total + stats[i]
    mean = total * (1.0 / (heads * HEAD * n_head))
    inverse = lax.rsqrt(mean[:blocks] + 1e-06)
    coef = mean[blocks:] * inverse * inverse

    def column(x, j):
        return jnp.broadcast_to(x[j : j + 1, :], (HEAD, HEAD)).T

    inverse = jnp.concatenate([column(inverse, j) for j in range(blocks)], axis=0)
    coef = jnp.concatenate([column(coef, j) for j in range(blocks)], axis=0)
    for h in range(heads):
        scaled = u[:, cols(h)].astype(F32) * gain_of(h)
        d = inverse * (scaled - att[:, cols(h)] * coef)
        d_low = d.astype(BF16)
        dfull[:, cols(h)] = d
        dlow[:, cols(h)] = d_low
        put_state(local2, h, nn(qt[h], d_low))
    scan2.to_mate()

    gains[0] = jnp.zeros((ROWS, HEAD), F32)
    for h in range(heads):
        normed = att[:, cols(h)] * inverse
        normed_out[:, cols(h)] = (normed * gain_of(h)).astype(BF16)
        gains[0, h : h + 1, :] = jnp.sum(
            u[:, cols(h)].astype(F32) * normed, axis=0, keepdims=True
        )

    to_mate = copy_to(gains.at[0], gains.at[3], send_sem.at[7], recv_sem.at[7], seq=mate)
    to_mate.start()
    scan2.to_owners()

    to_mate.wait_recv()
    gains[1] = gains[0] + gains[3]
    line_gains[pair] = gains[1]
    for offset in away[:-1]:
        copy_to(
            gains.at[1], line_gains.at[pair], send_sem.at[8], recv_sem.at[8],
            seq=device(line, pair_at(offset), side),
        ).start()

    def query_gradient(h):
        d_low = dlow[:, cols(h)]
        d_rest = (dfull[:, cols(h)] - d_low.astype(F32)).astype(BF16)
        high, low = halves(state_of(before, h))
        carried = nt(d_low, high) + (nt(d_low, low) + nt(d_rest, high))
        top, low = causal(d_low, v[:, cols(h)], k[:, cols(h)])
        qgrad_out[lo, cols(h)] = (top + carried[lo]).astype(BF16)
        qgrad_out[hi, cols(h)] = (low + carried[hi]).astype(BF16)

    for h in range(heads):
        query_gradient(h)

    totals[me] = scan2.add_up(jnp.zeros((ROWS, HEAD), F32))

    def send_total(j, carry):
        copy_to(
            totals.at[me], totals.at[me], send_sem.at[5], recv_sem.at[5],
            seq=line * PLANES + step_z(j),
        ).start()
        return carry

    lax.fori_loop(0, PLANES - 1, send_total, 0)
    scan2.to_blocks()

    for h in range(heads):
        top, low = anticausal(v[:, cols(h)], dlow[:, cols(h)], q[:, cols(h)])
        kpart[lo, cols(h)] = top
        kpart[hi, cols(h)] = low
        top, low = anticausal(k[:, cols(h)], q[:, cols(h)], dlow[:, cols(h)])
        vpart[lo, cols(h)] = top
        vpart[hi, cols(h)] = low

    some = totals.at[pl.ds(0, PLANES - 1)]
    copy_to(some, some, send_sem.at[5], recv_sem.at[5], seq=me).wait_recv()
    row = totals.at[pl.ds(line * PLANES, PLANES)]
    for i in (2, 1, 3):
        copy_to(
            row, row, send_sem.at[6], recv_sem.at[6], seq=device(line_at(i), pair, side)
        ).start()
    seven = line_gains.at[pl.ds(0, pairs - 1)]
    copy_to(seven, seven, send_sem.at[8], recv_sem.at[8], seq=me).wait_recv()
    gain = line_gains[0]
    for i in range(1, pairs):
        gain = gain + line_gains[i]
    gains[2] = gain
    all_gains[line] = gain
    for i in (2, 1, 3):
        copy_to(
            gains.at[2], all_gains.at[line], send_sem.at[9], recv_sem.at[9],
            seq=device(line_at(i), pair, side),
        ).start()

    def other_gradients(part):
        for i in range(heads // 2):
            at = pl.ds(pl.multiple_of((heads // 2 * part + i) * HEAD, HEAD), HEAD)
            rows_i = after[part, LINES * i : LINES * (i + 1)].reshape(HEAD, HEAD)
            high, low = halves(rows_i)
            vh, kh = v[:, at], k[:, at]
            kgrad_out[:, at] = (kpart[:, at] + (nt(vh, high) + nt(vh, low))).astype(BF16)
            vgrad_out[:, at] = (vpart[:, at] + (nn(kh, high) + nn(kh, low))).astype(BF16)

    scan2.to_mate_back()
    other_gradients(side)
    scan2.finish()
    other_gradients(1 - side)

    three = totals.at[pl.ds(0, (LINES - 1) * PLANES)]
    copy_to(three, three, send_sem.at[6], recv_sem.at[6], seq=me).wait_recv()
    for at in range(n_seq):
        owner = device(at % LINES, at % (n_seq // 2) // LINES, at // (n_seq // 2))
        state_out[at] = totals[owner]
    some_gains = all_gains.at[pl.ds(0, LINES - 1)]
    copy_to(some_gains, some_gains, send_sem.at[9], recv_sem.at[9], seq=me).wait_recv()
    gain = all_gains[0]
    for i in range(1, LINES):
        gain = gain + all_gains[i]
    gain_out[...] = gain[:heads]

    scan1.sent()
    scan2.sent()
    copy_to(others, others, send_sem.at[2], recv_sem.at[2], head=mine).wait_send()
    copy_to(some, some, send_sem.at[5], recv_sem.at[5], seq=me).wait_send()
    copy_to(three, three, send_sem.at[6], recv_sem.at[6], seq=me).wait_send()
    to_mate.wait_send()
    copy_to(seven, seven, send_sem.at[8], recv_sem.at[8], seq=me).wait_send()
    copy_to(some_gains, some_gains, send_sem.at[9], recv_sem.at[9], seq=me).wait_send()


def store_kernel(*refs):
    n = len(refs) // 2
    stores = []
    for i in range(n):
        cuts = 4 if i < 4 else 1
        rows = refs[i].shape[0] // cuts
        for c in range(cuts):
            at = pl.ds(c * rows, rows)
            stores.append(
                pltpu.make_async_copy(
                    refs[i].at[at], refs[n + i].at[at], refs[-1].at[len(stores)]
                )
            )
    for store in stores:
        store.start()
    for store in stores:
        store.wait()


def per_device(query_in, key_in, value_in, upstream, norm_gain, state_in):
    tokens, columns = query_in.shape
    heads = state_in.shape[0]
    n_seq = lax.axis_size("seq")
    n_head = lax.axis_size("head")
    wide = jax.ShapeDtypeStruct((tokens, columns), BF16)
    slices = (n_seq, ROWS, HEAD)
    vmem = pl.BlockSpec(memory_space=pltpu.VMEM)
    anywhere = pl.BlockSpec(memory_space=pl.ANY)
    hbm = pl.BlockSpec(memory_space=pltpu.HBM)
    low = pltpu.VMEM((tokens, columns), BF16)
    full = pltpu.VMEM((tokens, columns), F32)
    pairs = PLANES // 2
    whole = pltpu.VMEM((2, pairs, LINES, ROWS, HEAD), F32)
    half = pltpu.VMEM((pairs, LINES, ROWS, HEAD), F32)
    flat = pltpu.VMEM((pairs * LINES, ROWS, HEAD), F32)
    shapes = (
        wide, wide, wide, wide,
        jax.ShapeDtypeStruct((heads, HEAD), F32),
        jax.ShapeDtypeStruct(slices, F32),
    )
    outs = pl.pallas_call(
        kernel,
        name="attention_and_gradients",
        out_shape=shapes,
        in_specs=[hbm] * 6,
        out_specs=[vmem] * 6,
        scratch_shapes=[low] * 4
        + [pltpu.VMEM((heads, HEAD), F32), pltpu.VMEM(slices, F32)]
        + [pltpu.VMEM((heads, HEAD, tokens), BF16), full, full, low, full, full]
        + ([whole] * 2 + [half] * 2 + [flat] * 2 + [half] * 2) * 2
        + [
            pltpu.VMEM((n_head, ROWS, HEAD), F32),
            pltpu.VMEM(slices, F32),
            pltpu.VMEM((4, ROWS, HEAD), F32),
            pltpu.VMEM((pairs, ROWS, HEAD), F32),
            pltpu.VMEM((LINES, ROWS, HEAD), F32),
            pltpu.SemaphoreType.DMA((6,)),
            pltpu.SemaphoreType.DMA((10,)),
            pltpu.SemaphoreType.DMA((10,)),
            pltpu.SemaphoreType.DMA((8,)),
            pltpu.SemaphoreType.DMA((2 * (2 * pairs + 2),)),
        ],
        compiler_params=pltpu.CompilerParams(
            collective_id=0, has_side_effects=True, vmem_limit_bytes=51 << 20
        ),
    )(
        query_in, key_in, value_in, upstream,
        norm_gain.reshape(heads, HEAD), state_in.reshape(slices),
    )
    outs = pl.pallas_call(
        store_kernel,
        name="store",
        out_shape=shapes,
        in_specs=[anywhere] * 6,
        out_specs=[hbm] * 6,
        scratch_shapes=[pltpu.SemaphoreType.DMA((18,))],
        compiler_params=pltpu.CompilerParams(vmem_limit_bytes=1 << 20),
    )(*outs)
    return (
        outs[0], outs[1], outs[2], outs[3],
        outs[4].reshape(heads * HEAD), outs[5].reshape(state_in.shape),
    )


def solution(mesh):
    wide = P("seq", "head")
    return jax.shard_map(
        per_device,
        mesh=mesh,
        in_specs=(wide, wide, wide, wide, P("head"), P("head", None, None)),
        out_specs=(wide, wide, wide, wide, P("head"), P("head", None, None)),
        check_vma=False,
    )
```

```python
import functools

import jax
import jax.numpy as jnp
from jax import lax
from jax.experimental import pallas as pl
from jax.experimental.pallas import tpu as pltpu
from jax.sharding import PartitionSpec as P

F32 = jnp.float32
BF16 = jnp.bfloat16
MESH = pl.DeviceIdType.MESH
HEAD = 128
ROWS = 8
PLANES = 16
LINES = 4


def nn(a, b):
    return lax.dot_general(a, b, (((1,), (0,)), ((), ())), preferred_element_type=F32)


def nt(a, b):
    return lax.dot_general(a, b, (((1,), (1,)), ((), ())), preferred_element_type=F32)


def tn(a, b):
    return lax.dot_general(a, b, (((0,), (0,)), ((), ())), preferred_element_type=F32)


def halves(x):
    high = x.astype(BF16)
    return high, (x - high.astype(F32)).astype(BF16)


def copy_to(src, dst, send, recv, **where):
    return pltpu.make_async_remote_copy(
        src, dst, send, recv, device_id=where, device_id_type=MESH
    )


def kernel(
    q_in, k_in, v_in, u_in, gain_in, state_in,
    normed_out, qgrad_out, kgrad_out, vgrad_out, gain_out, state_out,
    q, k, v, u, gain_ref, state_ref, qt, att, dfull, dlow, kpart, vpart,
    local1, before, mate1, sums1, got1, part1, back1, share1,
    local2, after, mate2, sums2, got2, part2, back2, share2,
    stats, totals, gains, line_gains, all_gains,
    in_sem, send_sem, recv_sem, scan_send, scan_recv,
):
    n_seq = lax.axis_size("seq")
    n_head = lax.axis_size("head")
    me = lax.axis_index("seq")
    mine = lax.axis_index("head")
    plane = lax.rem(me, PLANES)
    line = me // PLANES
    tokens = q.shape[0]
    heads = q.shape[1] // HEAD
    half = tokens // 2

    loads = [
        pltpu.make_async_copy(src, dst, in_sem.at[i])
        for i, (src, dst) in enumerate(
            (
                (k_in, k), (v_in, v), (q_in, q),
                (u_in, u), (gain_in, gain_ref), (state_in, state_ref),
            )
        )
    ]
    for load in loads:
        load.start()

    def step_z(j):
        far = (j + 1) // 2
        away = PLANES // 2 + jnp.where(lax.rem(j, 2) == 1, -far, far)
        return lax.rem(plane + away, PLANES)

    pair, side = plane // 2, lax.rem(plane, 2)
    pairs = PLANES // 2
    mate = line * PLANES + 2 * pair + 1 - side
    away = [pairs // 2]
    for far in range(1, pairs // 2 + 1):
        away += [pairs // 2 - far, pairs // 2 + far]
    away = away[:pairs]

    def pair_at(offset):
        return lax.rem(pair + offset, pairs)

    def line_at(offset):
        return lax.rem(line + offset, LINES)

    def device(y, p, at_side):
        return y * PLANES + 2 * p + at_side

    barrier = pltpu.get_barrier_semaphore()
    for offset in away:
        for dy in (2, 1, 3, 0):
            if offset or dy:
                pl.semaphore_signal(
                    barrier, inc=1, device_id_type=MESH,
                    device_id={"seq": device(line_at(dy), pair_at(offset), side)},
                )
        pl.semaphore_signal(
            barrier, inc=1, device_id_type=MESH,
            device_id={"seq": device(line, pair_at(offset), 1 - side)},
        )
    for i in range(1, n_head):
        pl.semaphore_signal(
            barrier, inc=1, device_id={"head": lax.rem(mine + i, n_head)}, device_id_type=MESH
        )

    def cols(h):
        return slice(h * HEAD, (h + 1) * HEAD)

    def lower(x):
        r = lax.broadcasted_iota(jnp.int32, x.shape, 0)
        c = lax.broadcasted_iota(jnp.int32, x.shape, 1)
        return r >= c

    def upper(x):
        r = lax.broadcasted_iota(jnp.int32, x.shape, 0)
        c = lax.broadcasted_iota(jnp.int32, x.shape, 1)
        return r <= c

    lo, hi = slice(0, half), slice(half, tokens)

    def causal(a, b, c):
        s = nt(a[lo], b[lo])
        top = nn(jnp.where(lower(s), s, 0.0).astype(BF16), c[lo])
        s = nt(a[hi], b[hi])
        low = nn(jnp.where(lower(s), s, 0.0).astype(BF16), c[hi])
        low = low + nn(nt(a[hi], b[lo]).astype(BF16), c[lo])
        return top, low

    def anticausal(a, b, c):
        s = nt(a[hi], b[hi])
        low = nn(jnp.where(upper(s), s, 0.0).astype(BF16), c[hi])
        s = nt(a[lo], b[lo])
        top = nn(jnp.where(upper(s), s, 0.0).astype(BF16), c[lo])
        top = top + nn(nt(a[lo], b[hi]).astype(BF16), c[hi])
        return top, low

    def put_state(ref, h, value):
        first = LINES * (h % 2)
        ref[h // 2, first : first + LINES] = value.reshape(LINES, LINES, ROWS, HEAD)

    def state_of(ref, h):
        first = LINES * (h % 2)
        return ref[h // 2, first : first + LINES].reshape(HEAD, HEAD)

    loads[0].wait()
    loads[1].wait()
    for h in range(heads):
        kv = tn(k[:, cols(h)], v[:, cols(h)])
        put_state(local1, h, kv)
    for load in loads[2:]:
        load.wait()

    def forward_inside(h):
        top, low = causal(q[:, cols(h)], k[:, cols(h)], v[:, cols(h)])
        att[lo, cols(h)] = top
        att[hi, cols(h)] = low

    forward_inside(0)
    pl.semaphore_wait(barrier, n_seq // 2 - 1 + pairs + n_head - 1)

    class Scan:
        def __init__(self, local, result, other, sums, got, part, back, share, index, reverse):
            self.local, self.result, self.other, self.sums = local, result, other, sums
            self.got, self.part, self.back, self.share = got, part, back, share
            self.index, self.reverse = index, reverse

        def copy(self, src, dst, send, recv, to):
            return copy_to(
                src, dst, scan_send.at[4 * self.index + send],
                scan_recv.at[(2 * pairs + 2) * self.index + recv], seq=to,
            )

        def to_mate(self):
            for j, offset in enumerate(away):
                p = pair_at(offset)
                self.copy(self.local.at[1 - side, p], self.other.at[p], 0, j, mate).start()

        def to_owners(self):
            place = line * pairs + pair
            for j, offset in enumerate(away):
                p = pair_at(offset)
                chunk = self.other.at[p]
                self.copy(chunk, chunk, 0, j, mate).wait_recv()
                self.sums[p] = self.other[p] + self.local[side, p]
                for dy in (2, 1, 3, 0):
                    y = line_at(dy)
                    if offset or dy:
                        self.copy(
                            self.sums.at[p, y], self.got.at[place], 1, pairs, device(y, p, side)
                        ).start()
                    else:
                        self.got[place] = self.sums[p, y]

        def add_up(self, total):
            most = self.got.at[pl.ds(0, LINES * pairs - 1)]
            self.copy(most, most, 1, pairs, mate).wait_recv()
            order = range(LINES * pairs)
            for b in reversed(order) if self.reverse else order:
                self.part[b] = total
                total = total + self.got[b]
            return total

        def to_blocks(self):
            for offset in away:
                p = pair_at(offset)
                recv = pairs + 1 + (pairs - offset) % pairs
                for dy in (2, 1, 3, 0):
                    y = line_at(dy)
                    part = self.part.at[y * pairs + p]
                    if offset or dy:
                        self.copy(
                            part, self.back.at[pair, line], 2, recv, device(y, p, side)
                        ).start()
                    else:
                        self.back[pair, line] = self.part[y * pairs + p]

        def to_mate_back(self):
            second = side == (0 if self.reverse else 1)
            for offset in reversed(away):
                p = pair_at(offset)
                chunk = self.back.at[p] if offset else self.back.at[p, pl.ds(0, LINES - 1)]
                self.copy(chunk, chunk, 2, pairs + 1 + offset, mate).wait_recv()
                base = self.back[p]
                self.share[p] = base + jnp.where(second, 0.0, self.local[side, p])
                self.copy(
                    self.share.at[p], self.result.at[side, p], 3, 2 * pairs + 1, mate
                ).start()
                self.result[side, p] = base + jnp.where(second, self.other[p], 0.0)

        def finish(self):
            whole = self.result.at[0]
            self.copy(whole, whole, 3, 2 * pairs + 1, mate).wait_recv()

        def sent(self):
            whole = self.result.at[0]
            most = self.got.at[pl.ds(0, LINES * pairs - 1)]
            for send, ref in enumerate((whole, most, most, whole)):
                self.copy(ref, ref, send, 0, mate).wait_send()

    scan1 = Scan(local1, before, mate1, sums1, got1, part1, back1, share1, 0, False)
    scan2 = Scan(local2, after, mate2, sums2, got2, part2, back2, share2, 1, True)

    scan1.to_mate()
    forward_inside(1)
    scan1.to_owners()
    for h in range(heads):
        qt[h] = q[:, cols(h)].T
    forward_inside(2)
    scan1.add_up(state_ref[side * (n_seq // 2) + pair * LINES + line])
    scan1.to_blocks()
    forward_inside(3)
    scan1.to_mate_back()

    def gain_of(h):
        return gain_ref[h : h + 1, :]

    def forward_carried(part, squares, products):
        for i in range(heads // 2):
            h = heads // 2 * part + i
            at = pl.ds(pl.multiple_of(h * HEAD, HEAD), HEAD)
            high, low = halves(before[part, LINES * i : LINES * (i + 1)].reshape(HEAD, HEAD))
            a = att[:, at] + (nn(q[:, at], high) + nn(q[:, at], low))
            att[:, at] = a
            squares = squares + a * a
            products = products + a * (u[:, at].astype(F32) * gain_ref[pl.ds(h, 1), :])
        return squares, products

    nothing = jnp.zeros((tokens, HEAD), F32)
    squares, products = forward_carried(side, nothing, nothing)
    scan1.finish()
    squares, products = forward_carried(1 - side, squares, products)
    blocks = tokens // HEAD
    for j in range(blocks):
        rows_j = slice(j * HEAD, (j + 1) * HEAD)
        stats[mine, j : j + 1, :] = jnp.sum(squares[rows_j].T, axis=0, keepdims=True)
        stats[mine, blocks + j : blocks + j + 1, :] = jnp.sum(
            products[rows_j].T, axis=0, keepdims=True
        )
    for i in range(1, n_head):
        copy_to(
            stats.at[mine], stats.at[mine], send_sem.at[2], recv_sem.at[2],
            head=lax.rem(mine + i, n_head),
        ).start()
    others = stats.at[pl.ds(0, n_head - 1)]
    copy_to(others, others, send_sem.at[2], recv_sem.at[2], head=mine).wait_recv()
    total = stats[0]
    for i in range(1, n_head):
        total = total + stats[i]
    mean = total * (1.0 / (heads * HEAD * n_head))
    inverse = lax.rsqrt(mean[:blocks] + 1e-06)
    coef = mean[blocks:] * inverse * inverse

    def column(x, j):
        return jnp.broadcast_to(x[j : j + 1, :], (HEAD, HEAD)).T

    inverse = jnp.concatenate([column(inverse, j) for j in range(blocks)], axis=0)
    coef = jnp.concatenate([column(coef, j) for j in range(blocks)], axis=0)
    for h in range(heads):
        scaled = u[:, cols(h)].astype(F32) * gain_of(h)
        d = inverse * (scaled - att[:, cols(h)] * coef)
        d_low = d.astype(BF16)
        dfull[:, cols(h)] = d
        dlow[:, cols(h)] = d_low
        put_state(local2, h, nn(qt[h], d_low))
    scan2.to_mate()

    gains[0] = jnp.zeros((ROWS, HEAD), F32)
    for h in range(heads):
        normed = att[:, cols(h)] * inverse
        normed_out[:, cols(h)] = (normed * gain_of(h)).astype(BF16)
        gains[0, h : h + 1, :] = jnp.sum(
            u[:, cols(h)].astype(F32) * normed, axis=0, keepdims=True
        )

    to_mate = copy_to(gains.at[0], gains.at[3], send_sem.at[7], recv_sem.at[7], seq=mate)
    to_mate.start()
    scan2.to_owners()

    to_mate.wait_recv()
    gains[1] = gains[0] + gains[3]
    line_gains[pair] = gains[1]
    for offset in away[:-1]:
        copy_to(
            gains.at[1], line_gains.at[pair], send_sem.at[8], recv_sem.at[8],
            seq=device(line, pair_at(offset), side),
        ).start()

    def query_gradient(h):
        d_low = dlow[:, cols(h)]
        d_rest = (dfull[:, cols(h)] - d_low.astype(F32)).astype(BF16)
        high, low = halves(state_of(before, h))
        carried = nt(d_low, high) + (nt(d_low, low) + nt(d_rest, high))
        top, low = causal(d_low, v[:, cols(h)], k[:, cols(h)])
        qgrad_out[lo, cols(h)] = (top + carried[lo]).astype(BF16)
        qgrad_out[hi, cols(h)] = (low + carried[hi]).astype(BF16)

    for h in range(heads):
        query_gradient(h)

    totals[me] = scan2.add_up(jnp.zeros((ROWS, HEAD), F32))

    def send_total(j, carry):
        copy_to(
            totals.at[me], totals.at[me], send_sem.at[5], recv_sem.at[5],
            seq=line * PLANES + step_z(j),
        ).start()
        return carry

    lax.fori_loop(0, PLANES - 1, send_total, 0)
    scan2.to_blocks()

    for h in range(heads):
        top, low = anticausal(v[:, cols(h)], dlow[:, cols(h)], q[:, cols(h)])
        kpart[lo, cols(h)] = top
        kpart[hi, cols(h)] = low
        top, low = anticausal(k[:, cols(h)], q[:, cols(h)], dlow[:, cols(h)])
        vpart[lo, cols(h)] = top
        vpart[hi, cols(h)] = low

    some = totals.at[pl.ds(0, PLANES - 1)]
    copy_to(some, some, send_sem.at[5], recv_sem.at[5], seq=me).wait_recv()
    row = totals.at[pl.ds(line * PLANES, PLANES)]
    for i in (2, 1, 3):
        copy_to(
            row, row, send_sem.at[6], recv_sem.at[6], seq=device(line_at(i), pair, side)
        ).start()
    seven = line_gains.at[pl.ds(0, pairs - 1)]
    copy_to(seven, seven, send_sem.at[8], recv_sem.at[8], seq=me).wait_recv()
    gain = line_gains[0]
    for i in range(1, pairs):
        gain = gain + line_gains[i]
    gains[2] = gain
    all_gains[line] = gain
    for i in (2, 1, 3):
        copy_to(
            gains.at[2], all_gains.at[line], send_sem.at[9], recv_sem.at[9],
            seq=device(line_at(i), pair, side),
        ).start()

    def other_gradients(part):
        for i in range(heads // 2):
            at = pl.ds(pl.multiple_of((heads // 2 * part + i) * HEAD, HEAD), HEAD)
            rows_i = after[part, LINES * i : LINES * (i + 1)].reshape(HEAD, HEAD)
            high, low = halves(rows_i)
            vh, kh = v[:, at], k[:, at]
            kgrad_out[:, at] = (kpart[:, at] + (nt(vh, high) + nt(vh, low))).astype(BF16)
            vgrad_out[:, at] = (vpart[:, at] + (nn(kh, high) + nn(kh, low))).astype(BF16)

    scan2.to_mate_back()
    other_gradients(side)
    scan2.finish()
    other_gradients(1 - side)

    three = totals.at[pl.ds(0, (LINES - 1) * PLANES)]
    copy_to(three, three, send_sem.at[6], recv_sem.at[6], seq=me).wait_recv()
    for at in range(n_seq):
        owner = device(at % LINES, at % (n_seq // 2) // LINES, at // (n_seq // 2))
        state_out[at] = totals[owner]
    some_gains = all_gains.at[pl.ds(0, LINES - 1)]
    copy_to(some_gains, some_gains, send_sem.at[9], recv_sem.at[9], seq=me).wait_recv()
    gain = all_gains[0]
    for i in range(1, LINES):
        gain = gain + all_gains[i]
    gain_out[...] = gain[:heads]

    scan1.sent()
    scan2.sent()
    copy_to(others, others, send_sem.at[2], recv_sem.at[2], head=mine).wait_send()
    copy_to(some, some, send_sem.at[5], recv_sem.at[5], seq=me).wait_send()
    copy_to(three, three, send_sem.at[6], recv_sem.at[6], seq=me).wait_send()
    to_mate.wait_send()
    copy_to(seven, seven, send_sem.at[8], recv_sem.at[8], seq=me).wait_send()
    copy_to(some_gains, some_gains, send_sem.at[9], recv_sem.at[9], seq=me).wait_send()


def store_kernel(*refs):
    n = len(refs) // 2
    stores = []
    for i in range(n):
        cuts = 1
        rows = refs[i].shape[0] // cuts
        for c in range(cuts):
            at = pl.ds(c * rows, rows)
            stores.append(
                pltpu.make_async_copy(
                    refs[i].at[at], refs[n + i].at[at], refs[-1].at[len(stores)]
                )
            )
    for store in stores:
        store.start()
    for store in stores:
        store.wait()


def per_device(query_in, key_in, value_in, upstream, norm_gain, state_in):
    tokens, columns = query_in.shape
    heads = state_in.shape[0]
    n_seq = lax.axis_size("seq")
    n_head = lax.axis_size("head")
    wide = jax.ShapeDtypeStruct((tokens, columns), BF16)
    slices = (n_seq, ROWS, HEAD)
    vmem = pl.BlockSpec(memory_space=pltpu.VMEM)
    anywhere = pl.BlockSpec(memory_space=pl.ANY)
    hbm = pl.BlockSpec(memory_space=pltpu.HBM)
    low = pltpu.VMEM((tokens, columns), BF16)
    full = pltpu.VMEM((tokens, columns), F32)
    pairs = PLANES // 2
    whole = pltpu.VMEM((2, pairs, LINES, ROWS, HEAD), F32)
    half = pltpu.VMEM((pairs, LINES, ROWS, HEAD), F32)
    flat = pltpu.VMEM((pairs * LINES, ROWS, HEAD), F32)
    shapes = (
        wide, wide, wide, wide,
        jax.ShapeDtypeStruct((heads, HEAD), F32),
        jax.ShapeDtypeStruct(slices, F32),
    )
    outs = pl.pallas_call(
        kernel,
        name="attention_and_gradients",
        out_shape=shapes,
        in_specs=[hbm] * 6,
        out_specs=[vmem] * 6,
        scratch_shapes=[low] * 4
        + [pltpu.VMEM((heads, HEAD), F32), pltpu.VMEM(slices, F32)]
        + [pltpu.VMEM((heads, HEAD, tokens), BF16), full, full, low, full, full]
        + ([whole] * 2 + [half] * 2 + [flat] * 2 + [half] * 2) * 2
        + [
            pltpu.VMEM((n_head, ROWS, HEAD), F32),
            pltpu.VMEM(slices, F32),
            pltpu.VMEM((4, ROWS, HEAD), F32),
            pltpu.VMEM((pairs, ROWS, HEAD), F32),
            pltpu.VMEM((LINES, ROWS, HEAD), F32),
            pltpu.SemaphoreType.DMA((6,)),
            pltpu.SemaphoreType.DMA((10,)),
            pltpu.SemaphoreType.DMA((10,)),
            pltpu.SemaphoreType.DMA((8,)),
            pltpu.SemaphoreType.DMA((2 * (2 * pairs + 2),)),
        ],
        compiler_params=pltpu.CompilerParams(
            collective_id=0, has_side_effects=True, vmem_limit_bytes=51 << 20
        ),
    )(
        *(
            pltpu.with_memory_space_constraint(x, pltpu.HBM)
            for x in (
                query_in, key_in, value_in, upstream,
                norm_gain.reshape(heads, HEAD), state_in.reshape(slices),
            )
        )
    )
    outs = pl.pallas_call(
        store_kernel,
        name="store",
        out_shape=shapes,
        in_specs=[anywhere] * 6,
        out_specs=[hbm] * 6,
        scratch_shapes=[pltpu.SemaphoreType.DMA((6,))],
        compiler_params=pltpu.CompilerParams(vmem_limit_bytes=1 << 20),
    )(*outs)
    return (
        outs[0], outs[1], outs[2], outs[3],
        outs[4].reshape(heads * HEAD), outs[5].reshape(state_in.shape),
    )


def solution(mesh):
    wide = P("seq", "head")
    return jax.shard_map(
        per_device,
        mesh=mesh,
        in_specs=(wide, wide, wide, wide, P("head"), P("head", None, None)),
        out_specs=(wide, wide, wide, wide, P("head"), P("head", None, None)),
        check_vma=False,
    )
```

```python
import functools

import jax
import jax.numpy as jnp
from jax import lax
from jax.experimental import pallas as pl
from jax.experimental.pallas import tpu as pltpu
from jax.sharding import PartitionSpec as P

F32 = jnp.float32
BF16 = jnp.bfloat16
MESH = pl.DeviceIdType.MESH
HEAD = 128
ROWS = 8
PLANES = 16
LINES = 4


def nn(a, b):
    return lax.dot_general(a, b, (((1,), (0,)), ((), ())), preferred_element_type=F32)


def nt(a, b):
    return lax.dot_general(a, b, (((1,), (1,)), ((), ())), preferred_element_type=F32)


def tn(a, b):
    return lax.dot_general(a, b, (((0,), (0,)), ((), ())), preferred_element_type=F32)


def halves(x):
    high = x.astype(BF16)
    return high, (x - high.astype(F32)).astype(BF16)


def copy_to(src, dst, send, recv, **where):
    return pltpu.make_async_remote_copy(
        src, dst, send, recv, device_id=where, device_id_type=MESH
    )


def kernel(
    q_in, k_in, v_in, u_in, gain_in, state_in,
    normed_out, qgrad_out, kgrad_out, vgrad_out, gain_out, state_out,
    q, k, v, u, gain_ref, state_ref, qt, att, dfull, dlow, kpart, vpart,
    local1, before, mate1, sums1, got1, part1, back1, share1,
    local2, after, mate2, sums2, got2, part2, back2, share2,
    stats, totals, gains, line_gains, all_gains,
    in_sem, send_sem, recv_sem, scan_send, scan_recv,
):
    n_seq = lax.axis_size("seq")
    n_head = lax.axis_size("head")
    me = lax.axis_index("seq")
    mine = lax.axis_index("head")
    plane = lax.rem(me, PLANES)
    line = me // PLANES
    tokens = q.shape[0]
    heads = q.shape[1] // HEAD
    half = tokens // 2

    loads = [
        pltpu.make_async_copy(src, dst, in_sem.at[i])
        for i, (src, dst) in enumerate(
            (
                (k_in, k), (v_in, v), (q_in, q),
                (u_in, u), (gain_in, gain_ref), (state_in, state_ref),
            )
        )
    ]
    for load in loads:
        load.start()

    def step_z(j):
        far = (j + 1) // 2
        away = PLANES // 2 + jnp.where(lax.rem(j, 2) == 1, -far, far)
        return lax.rem(plane + away, PLANES)

    pair, side = plane // 2, lax.rem(plane, 2)
    pairs = PLANES // 2
    mate = line * PLANES + 2 * pair + 1 - side
    away = [pairs // 2]
    for far in range(1, pairs // 2 + 1):
        away += [pairs // 2 - far, pairs // 2 + far]
    away = away[:pairs]

    def pair_at(offset):
        return lax.rem(pair + offset, pairs)

    def line_at(offset):
        return lax.rem(line + offset, LINES)

    def device(y, p, at_side):
        return y * PLANES + 2 * p + at_side

    barrier = pltpu.get_barrier_semaphore()
    for offset in away:
        for dy in (2, 1, 3, 0):
            if offset or dy:
                pl.semaphore_signal(
                    barrier, inc=1, device_id_type=MESH,
                    device_id={"seq": device(line_at(dy), pair_at(offset), side)},
                )
        pl.semaphore_signal(
            barrier, inc=1, device_id_type=MESH,
            device_id={"seq": device(line, pair_at(offset), 1 - side)},
        )
    for i in range(1, n_head):
        pl.semaphore_signal(
            barrier, inc=1, device_id={"head": lax.rem(mine + i, n_head)}, device_id_type=MESH
        )

    def cols(h):
        return slice(h * HEAD, (h + 1) * HEAD)

    def lower(x):
        r = lax.broadcasted_iota(jnp.int32, x.shape, 0)
        c = lax.broadcasted_iota(jnp.int32, x.shape, 1)
        return r >= c

    def upper(x):
        r = lax.broadcasted_iota(jnp.int32, x.shape, 0)
        c = lax.broadcasted_iota(jnp.int32, x.shape, 1)
        return r <= c

    lo, hi = slice(0, half), slice(half, tokens)

    def causal(a, b, c):
        s = nt(a[lo], b[lo])
        top = nn(jnp.where(lower(s), s, 0.0).astype(BF16), c[lo])
        s = nt(a[hi], b[hi])
        low = nn(jnp.where(lower(s), s, 0.0).astype(BF16), c[hi])
        low = low + nn(nt(a[hi], b[lo]).astype(BF16), c[lo])
        return top, low

    def anticausal(a, b, c):
        s = nt(a[hi], b[hi])
        low = nn(jnp.where(upper(s), s, 0.0).astype(BF16), c[hi])
        s = nt(a[lo], b[lo])
        top = nn(jnp.where(upper(s), s, 0.0).astype(BF16), c[lo])
        top = top + nn(nt(a[lo], b[hi]).astype(BF16), c[hi])
        return top, low

    def put_state(ref, h, value):
        first = LINES * (h % 2)
        ref[h // 2, first : first + LINES] = value.reshape(LINES, LINES, ROWS, HEAD)

    def state_of(ref, h):
        first = LINES * (h % 2)
        return ref[h // 2, first : first + LINES].reshape(HEAD, HEAD)

    loads[0].wait()
    loads[1].wait()
    for h in range(heads):
        kv = tn(k[:, cols(h)], v[:, cols(h)])
        put_state(local1, h, kv)
    for load in loads[2:]:
        load.wait()

    def forward_inside(h):
        top, low = causal(q[:, cols(h)], k[:, cols(h)], v[:, cols(h)])
        att[lo, cols(h)] = top
        att[hi, cols(h)] = low

    forward_inside(0)
    pl.semaphore_wait(barrier, n_seq // 2 - 1 + pairs + n_head - 1)

    class Scan:
        def __init__(self, local, result, other, sums, got, part, back, share, index, reverse):
            self.local, self.result, self.other, self.sums = local, result, other, sums
            self.got, self.part, self.back, self.share = got, part, back, share
            self.index, self.reverse = index, reverse

        def copy(self, src, dst, send, recv, to):
            return copy_to(
                src, dst, scan_send.at[4 * self.index + send],
                scan_recv.at[(2 * pairs + 2) * self.index + recv], seq=to,
            )

        def to_mate(self):
            for j, offset in enumerate(away):
                p = pair_at(offset)
                self.copy(self.local.at[1 - side, p], self.other.at[p], 0, j, mate).start()

        def to_owners(self):
            place = line * pairs + pair
            for j, offset in enumerate(away):
                p = pair_at(offset)
                chunk = self.other.at[p]
                self.copy(chunk, chunk, 0, j, mate).wait_recv()
                self.sums[p] = self.other[p] + self.local[side, p]
                for dy in (2, 1, 3, 0):
                    y = line_at(dy)
                    if offset or dy:
                        self.copy(
                            self.sums.at[p, y], self.got.at[place], 1, pairs, device(y, p, side)
                        ).start()
                    else:
                        self.got[place] = self.sums[p, y]

        def add_up(self, total):
            most = self.got.at[pl.ds(0, LINES * pairs - 1)]
            self.copy(most, most, 1, pairs, mate).wait_recv()
            order = range(LINES * pairs)
            for b in reversed(order) if self.reverse else order:
                self.part[b] = total
                total = total + self.got[b]
            return total

        def to_blocks(self):
            for offset in away:
                p = pair_at(offset)
                recv = pairs + 1 + (pairs - offset) % pairs
                for dy in (2, 1, 3, 0):
                    y = line_at(dy)
                    part = self.part.at[y * pairs + p]
                    if offset or dy:
                        self.copy(
                            part, self.back.at[pair, line], 2, recv, device(y, p, side)
                        ).start()
                    else:
                        self.back[pair, line] = self.part[y * pairs + p]

        def to_mate_back(self, offsets):
            second = side == (0 if self.reverse else 1)
            for offset in offsets:
                p = pair_at(offset)
                chunk = self.back.at[p] if offset else self.back.at[p, pl.ds(0, LINES - 1)]
                self.copy(chunk, chunk, 2, pairs + 1 + offset, mate).wait_recv()
                base = self.back[p]
                self.share[p] = base + jnp.where(second, 0.0, self.local[side, p])
                self.copy(
                    self.share.at[p], self.result.at[side, p], 3, 2 * pairs + 1, mate
                ).start()
                self.result[side, p] = base + jnp.where(second, self.other[p], 0.0)

        def finish(self):
            whole = self.result.at[0]
            self.copy(whole, whole, 3, 2 * pairs + 1, mate).wait_recv()

        def sent(self):
            whole = self.result.at[0]
            most = self.got.at[pl.ds(0, LINES * pairs - 1)]
            for send, ref in enumerate((whole, most, most, whole)):
                self.copy(ref, ref, send, 0, mate).wait_send()

    scan1 = Scan(local1, before, mate1, sums1, got1, part1, back1, share1, 0, False)
    scan2 = Scan(local2, after, mate2, sums2, got2, part2, back2, share2, 1, True)

    scan1.to_mate()
    forward_inside(1)
    scan1.to_owners()
    for h in range(heads):
        qt[h] = q[:, cols(h)].T
    forward_inside(2)
    scan1.add_up(state_ref[side * (n_seq // 2) + pair * LINES + line])
    scan1.to_blocks()
    forward_inside(3)
    scan1.to_mate_back(away[::-1])

    def gain_of(h):
        return gain_ref[h : h + 1, :]

    def forward_carried(part, squares, products):
        for i in range(heads // 2):
            h = heads // 2 * part + i
            at = pl.ds(pl.multiple_of(h * HEAD, HEAD), HEAD)
            high, low = halves(before[part, LINES * i : LINES * (i + 1)].reshape(HEAD, HEAD))
            a = att[:, at] + (nn(q[:, at], high) + nn(q[:, at], low))
            att[:, at] = a
            squares = squares + a * a
            products = products + a * (u[:, at].astype(F32) * gain_ref[pl.ds(h, 1), :])
        return squares, products

    nothing = jnp.zeros((tokens, HEAD), F32)
    squares, products = forward_carried(side, nothing, nothing)
    scan1.finish()
    squares, products = forward_carried(1 - side, squares, products)
    blocks = tokens // HEAD
    for j in range(blocks):
        rows_j = slice(j * HEAD, (j + 1) * HEAD)
        stats[mine, j : j + 1, :] = jnp.sum(squares[rows_j].T, axis=0, keepdims=True)
        stats[mine, blocks + j : blocks + j + 1, :] = jnp.sum(
            products[rows_j].T, axis=0, keepdims=True
        )
    for i in range(1, n_head):
        copy_to(
            stats.at[mine], stats.at[mine], send_sem.at[2], recv_sem.at[2],
            head=lax.rem(mine + i, n_head),
        ).start()
    others = stats.at[pl.ds(0, n_head - 1)]
    copy_to(others, others, send_sem.at[2], recv_sem.at[2], head=mine).wait_recv()
    total = stats[0]
    for i in range(1, n_head):
        total = total + stats[i]
    mean = total * (1.0 / (heads * HEAD * n_head))
    inverse = lax.rsqrt(mean[:blocks] + 1e-06)
    coef = mean[blocks:] * inverse * inverse

    def column(x, j):
        return jnp.broadcast_to(x[j : j + 1, :], (HEAD, HEAD)).T

    inverse = jnp.concatenate([column(inverse, j) for j in range(blocks)], axis=0)
    coef = jnp.concatenate([column(coef, j) for j in range(blocks)], axis=0)
    for h in range(heads):
        scaled = u[:, cols(h)].astype(F32) * gain_of(h)
        d = inverse * (scaled - att[:, cols(h)] * coef)
        d_low = d.astype(BF16)
        dfull[:, cols(h)] = d
        dlow[:, cols(h)] = d_low
        put_state(local2, h, nn(qt[h], d_low))
    scan2.to_mate()

    gains[0] = jnp.zeros((ROWS, HEAD), F32)
    for h in range(heads):
        normed = att[:, cols(h)] * inverse
        normed_out[:, cols(h)] = (normed * gain_of(h)).astype(BF16)
        gains[0, h : h + 1, :] = jnp.sum(
            u[:, cols(h)].astype(F32) * normed, axis=0, keepdims=True
        )

    to_mate = copy_to(gains.at[0], gains.at[3], send_sem.at[7], recv_sem.at[7], seq=mate)
    to_mate.start()
    scan2.to_owners()

    to_mate.wait_recv()
    gains[1] = gains[0] + gains[3]
    line_gains[pair] = gains[1]
    for offset in away[:-1]:
        copy_to(
            gains.at[1], line_gains.at[pair], send_sem.at[8], recv_sem.at[8],
            seq=device(line, pair_at(offset), side),
        ).start()

    def query_gradient(h):
        d_low = dlow[:, cols(h)]
        d_rest = (dfull[:, cols(h)] - d_low.astype(F32)).astype(BF16)
        high, low = halves(state_of(before, h))
        carried = nt(d_low, high) + (nt(d_low, low) + nt(d_rest, high))
        top, low = causal(d_low, v[:, cols(h)], k[:, cols(h)])
        qgrad_out[lo, cols(h)] = (top + carried[lo]).astype(BF16)
        qgrad_out[hi, cols(h)] = (low + carried[hi]).astype(BF16)

    for h in range(heads):
        query_gradient(h)

    totals[me] = scan2.add_up(jnp.zeros((ROWS, HEAD), F32))

    def send_total(j, carry):
        copy_to(
            totals.at[me], totals.at[me], send_sem.at[5], recv_sem.at[5],
            seq=line * PLANES + step_z(j),
        ).start()
        return carry

    lax.fori_loop(0, PLANES - 1, send_total, 0)
    scan2.to_blocks()

    for h in range(heads):
        top, low = anticausal(v[:, cols(h)], dlow[:, cols(h)], q[:, cols(h)])
        kpart[lo, cols(h)] = top
        kpart[hi, cols(h)] = low
        top, low = anticausal(k[:, cols(h)], q[:, cols(h)], dlow[:, cols(h)])
        vpart[lo, cols(h)] = top
        vpart[hi, cols(h)] = low

    scan2.to_mate_back(away[pairs // 2 :][::-1])
    some = totals.at[pl.ds(0, PLANES - 1)]
    copy_to(some, some, send_sem.at[5], recv_sem.at[5], seq=me).wait_recv()
    row = totals.at[pl.ds(line * PLANES, PLANES)]
    for i in (2, 1, 3):
        copy_to(
            row, row, send_sem.at[6], recv_sem.at[6], seq=device(line_at(i), pair, side)
        ).start()
    seven = line_gains.at[pl.ds(0, pairs - 1)]
    copy_to(seven, seven, send_sem.at[8], recv_sem.at[8], seq=me).wait_recv()
    gain = line_gains[0]
    for i in range(1, pairs):
        gain = gain + line_gains[i]
    gains[2] = gain
    all_gains[line] = gain
    for i in (2, 1, 3):
        copy_to(
            gains.at[2], all_gains.at[line], send_sem.at[9], recv_sem.at[9],
            seq=device(line_at(i), pair, side),
        ).start()

    def other_gradients(part):
        for i in range(heads // 2):
            at = pl.ds(pl.multiple_of((heads // 2 * part + i) * HEAD, HEAD), HEAD)
            rows_i = after[part, LINES * i : LINES * (i + 1)].reshape(HEAD, HEAD)
            high, low = halves(rows_i)
            vh, kh = v[:, at], k[:, at]
            kgrad_out[:, at] = (kpart[:, at] + (nt(vh, high) + nt(vh, low))).astype(BF16)
            vgrad_out[:, at] = (vpart[:, at] + (nn(kh, high) + nn(kh, low))).astype(BF16)

    scan2.to_mate_back(away[: pairs // 2][::-1])
    other_gradients(side)
    scan2.finish()
    other_gradients(1 - side)

    three = totals.at[pl.ds(0, (LINES - 1) * PLANES)]
    copy_to(three, three, send_sem.at[6], recv_sem.at[6], seq=me).wait_recv()
    for at in range(n_seq):
        owner = device(at % LINES, at % (n_seq // 2) // LINES, at // (n_seq // 2))
        state_out[at] = totals[owner]
    some_gains = all_gains.at[pl.ds(0, LINES - 1)]
    copy_to(some_gains, some_gains, send_sem.at[9], recv_sem.at[9], seq=me).wait_recv()
    gain = all_gains[0]
    for i in range(1, LINES):
        gain = gain + all_gains[i]
    gain_out[...] = gain[:heads]

    scan1.sent()
    scan2.sent()
    copy_to(others, others, send_sem.at[2], recv_sem.at[2], head=mine).wait_send()
    copy_to(some, some, send_sem.at[5], recv_sem.at[5], seq=me).wait_send()
    copy_to(three, three, send_sem.at[6], recv_sem.at[6], seq=me).wait_send()
    to_mate.wait_send()
    copy_to(seven, seven, send_sem.at[8], recv_sem.at[8], seq=me).wait_send()
    copy_to(some_gains, some_gains, send_sem.at[9], recv_sem.at[9], seq=me).wait_send()


def store_kernel(*refs):
    n = len(refs) // 2
    stores = []
    for i in range(n):
        cuts = 1
        rows = refs[i].shape[0] // cuts
        for c in range(cuts):
            at = pl.ds(c * rows, rows)
            stores.append(
                pltpu.make_async_copy(
                    refs[i].at[at], refs[n + i].at[at], refs[-1].at[len(stores)]
                )
            )
    for store in stores:
        store.start()
    for store in stores:
        store.wait()


def per_device(query_in, key_in, value_in, upstream, norm_gain, state_in):
    tokens, columns = query_in.shape
    heads = state_in.shape[0]
    n_seq = lax.axis_size("seq")
    n_head = lax.axis_size("head")
    wide = jax.ShapeDtypeStruct((tokens, columns), BF16)
    slices = (n_seq, ROWS, HEAD)
    vmem = pl.BlockSpec(memory_space=pltpu.VMEM)
    anywhere = pl.BlockSpec(memory_space=pl.ANY)
    hbm = pl.BlockSpec(memory_space=pltpu.HBM)
    low = pltpu.VMEM((tokens, columns), BF16)
    full = pltpu.VMEM((tokens, columns), F32)
    pairs = PLANES // 2
    whole = pltpu.VMEM((2, pairs, LINES, ROWS, HEAD), F32)
    half = pltpu.VMEM((pairs, LINES, ROWS, HEAD), F32)
    flat = pltpu.VMEM((pairs * LINES, ROWS, HEAD), F32)
    shapes = (
        wide, wide, wide, wide,
        jax.ShapeDtypeStruct((heads, HEAD), F32),
        jax.ShapeDtypeStruct(slices, F32),
    )
    outs = pl.pallas_call(
        kernel,
        name="attention_and_gradients",
        out_shape=shapes,
        in_specs=[hbm] * 6,
        out_specs=[vmem] * 6,
        scratch_shapes=[low] * 4
        + [pltpu.VMEM((heads, HEAD), F32), pltpu.VMEM(slices, F32)]
        + [pltpu.VMEM((heads, HEAD, tokens), BF16), full, full, low, full, full]
        + ([whole] * 2 + [half] * 2 + [flat] * 2 + [half] * 2) * 2
        + [
            pltpu.VMEM((n_head, ROWS, HEAD), F32),
            pltpu.VMEM(slices, F32),
            pltpu.VMEM((4, ROWS, HEAD), F32),
            pltpu.VMEM((pairs, ROWS, HEAD), F32),
            pltpu.VMEM((LINES, ROWS, HEAD), F32),
            pltpu.SemaphoreType.DMA((6,)),
            pltpu.SemaphoreType.DMA((10,)),
            pltpu.SemaphoreType.DMA((10,)),
            pltpu.SemaphoreType.DMA((8,)),
            pltpu.SemaphoreType.DMA((2 * (2 * pairs + 2),)),
        ],
        compiler_params=pltpu.CompilerParams(
            collective_id=0, has_side_effects=True, vmem_limit_bytes=51 << 20
        ),
    )(
        *(
            pltpu.with_memory_space_constraint(x, pltpu.HBM)
            for x in (
                query_in, key_in, value_in, upstream,
                norm_gain.reshape(heads, HEAD), state_in.reshape(slices),
            )
        )
    )
    outs = pl.pallas_call(
        store_kernel,
        name="store",
        out_shape=shapes,
        in_specs=[anywhere] * 6,
        out_specs=[hbm] * 6,
        scratch_shapes=[pltpu.SemaphoreType.DMA((6,))],
        compiler_params=pltpu.CompilerParams(vmem_limit_bytes=1 << 20),
    )(*outs)
    return (
        outs[0], outs[1], outs[2], outs[3],
        outs[4].reshape(heads * HEAD), outs[5].reshape(state_in.shape),
    )


def solution(mesh):
    wide = P("seq", "head")
    return jax.shard_map(
        per_device,
        mesh=mesh,
        in_specs=(wide, wide, wide, wide, P("head"), P("head", None, None)),
        out_specs=(wide, wide, wide, wide, P("head"), P("head", None, None)),
        check_vma=False,
    )
```

```python
import functools

import jax
import jax.numpy as jnp
from jax import lax
from jax.experimental import pallas as pl
from jax.experimental.pallas import tpu as pltpu
from jax.sharding import PartitionSpec as P

F32 = jnp.float32
BF16 = jnp.bfloat16
MESH = pl.DeviceIdType.MESH
HEAD = 128
ROWS = 8
PLANES = 16
LINES = 4


def nn(a, b):
    return lax.dot_general(a, b, (((1,), (0,)), ((), ())), preferred_element_type=F32)


def nt(a, b):
    return lax.dot_general(a, b, (((1,), (1,)), ((), ())), preferred_element_type=F32)


def tn(a, b):
    return lax.dot_general(a, b, (((0,), (0,)), ((), ())), preferred_element_type=F32)


def halves(x):
    high = x.astype(BF16)
    return high, (x - high.astype(F32)).astype(BF16)


def copy_to(src, dst, send, recv, **where):
    return pltpu.make_async_remote_copy(
        src, dst, send, recv, device_id=where, device_id_type=MESH
    )


def kernel(
    q_in, k_in, v_in, u_in, gain_in, state_in,
    normed_out, qgrad_out, kgrad_out, vgrad_out, gain_out, state_out,
    q, k, v, u, gain_ref, state_ref, qt, att, dfull, dlow, kpart, vpart,
    local1, before, mate1, sums1, got1, part1, back1, share1,
    local2, after, mate2, sums2, got2, part2, back2, share2,
    stats, totals, gains, line_gains, all_gains,
    in_sem, send_sem, recv_sem, scan_send, scan_recv,
):
    n_seq = lax.axis_size("seq")
    n_head = lax.axis_size("head")
    me = lax.axis_index("seq")
    mine = lax.axis_index("head")
    plane = lax.rem(me, PLANES)
    line = me // PLANES
    tokens = q.shape[0]
    heads = q.shape[1] // HEAD
    half = tokens // 2

    loads = [
        pltpu.make_async_copy(src, dst, in_sem.at[i])
        for i, (src, dst) in enumerate(
            (
                (k_in, k), (v_in, v), (q_in, q),
                (u_in, u), (gain_in, gain_ref), (state_in, state_ref),
            )
        )
    ]
    for load in loads:
        load.start()

    def step_z(j):
        far = (j + 1) // 2
        away = PLANES // 2 + jnp.where(lax.rem(j, 2) == 1, -far, far)
        return lax.rem(plane + away, PLANES)

    pair, side = plane // 2, lax.rem(plane, 2)
    pairs = PLANES // 2
    mate = line * PLANES + 2 * pair + 1 - side
    away = [pairs // 2]
    for far in range(1, pairs // 2 + 1):
        away += [pairs // 2 - far, pairs // 2 + far]
    away = away[:pairs]

    def pair_at(offset):
        return lax.rem(pair + offset, pairs)

    def line_at(offset):
        return lax.rem(line + offset, LINES)

    def device(y, p, at_side):
        return y * PLANES + 2 * p + at_side

    barrier = pltpu.get_barrier_semaphore()
    for offset in away:
        for dy in (2, 1, 3, 0):
            if offset or dy:
                pl.semaphore_signal(
                    barrier, inc=1, device_id_type=MESH,
                    device_id={"seq": device(line_at(dy), pair_at(offset), side)},
                )
        pl.semaphore_signal(
            barrier, inc=1, device_id_type=MESH,
            device_id={"seq": device(line, pair_at(offset), 1 - side)},
        )
    for i in range(1, n_head):
        pl.semaphore_signal(
            barrier, inc=1, device_id={"head": lax.rem(mine + i, n_head)}, device_id_type=MESH
        )

    def cols(h):
        return slice(h * HEAD, (h + 1) * HEAD)

    def lower(x):
        r = lax.broadcasted_iota(jnp.int32, x.shape, 0)
        c = lax.broadcasted_iota(jnp.int32, x.shape, 1)
        return r >= c

    def upper(x):
        r = lax.broadcasted_iota(jnp.int32, x.shape, 0)
        c = lax.broadcasted_iota(jnp.int32, x.shape, 1)
        return r <= c

    lo, hi = slice(0, half), slice(half, tokens)

    def causal(a, b, c):
        s = nt(a[lo], b[lo])
        top = nn(jnp.where(lower(s), s, 0.0).astype(BF16), c[lo])
        s = nt(a[hi], b[hi])
        low = nn(jnp.where(lower(s), s, 0.0).astype(BF16), c[hi])
        low = low + nn(nt(a[hi], b[lo]).astype(BF16), c[lo])
        return top, low

    def anticausal(a, b, c):
        s = nt(a[hi], b[hi])
        low = nn(jnp.where(upper(s), s, 0.0).astype(BF16), c[hi])
        s = nt(a[lo], b[lo])
        top = nn(jnp.where(upper(s), s, 0.0).astype(BF16), c[lo])
        top = top + nn(nt(a[lo], b[hi]).astype(BF16), c[hi])
        return top, low

    def put_state(ref, h, value):
        first = LINES * (h % 2)
        ref[h // 2, first : first + LINES] = value.reshape(LINES, LINES, ROWS, HEAD)

    def state_of(ref, h):
        first = LINES * (h % 2)
        return ref[h // 2, first : first + LINES].reshape(HEAD, HEAD)

    loads[0].wait()
    loads[1].wait()
    for h in range(heads):
        kv = tn(k[:, cols(h)], v[:, cols(h)])
        put_state(local1, h, kv)
    for load in loads[2:]:
        load.wait()

    def forward_inside(h):
        top, low = causal(q[:, cols(h)], k[:, cols(h)], v[:, cols(h)])
        att[lo, cols(h)] = top
        att[hi, cols(h)] = low

    forward_inside(0)
    pl.semaphore_wait(barrier, n_seq // 2 - 1 + pairs + n_head - 1)

    class Scan:
        def __init__(self, local, result, other, sums, got, part, back, share, index, reverse):
            self.local, self.result, self.other, self.sums = local, result, other, sums
            self.got, self.part, self.back, self.share = got, part, back, share
            self.index, self.reverse = index, reverse

        def copy(self, src, dst, send, recv, to):
            return copy_to(
                src, dst, scan_send.at[4 * self.index + send],
                scan_recv.at[(2 * pairs + 2) * self.index + recv], seq=to,
            )

        def to_mate(self):
            for j, offset in enumerate(away):
                p = pair_at(offset)
                self.copy(self.local.at[1 - side, p], self.other.at[p], 0, j, mate).start()

        def to_owners(self):
            place = line * pairs + pair
            for j, offset in enumerate(away):
                p = pair_at(offset)
                chunk = self.other.at[p]
                self.copy(chunk, chunk, 0, j, mate).wait_recv()
                self.sums[p] = self.other[p] + self.local[side, p]
                for dy in (2, 1, 3, 0):
                    y = line_at(dy)
                    if offset or dy:
                        self.copy(
                            self.sums.at[p, y], self.got.at[place], 1, pairs, device(y, p, side)
                        ).start()
                    else:
                        self.got[place] = self.sums[p, y]

        def add_up(self, total):
            most = self.got.at[pl.ds(0, LINES * pairs - 1)]
            self.copy(most, most, 1, pairs, mate).wait_recv()
            order = range(LINES * pairs)
            for b in reversed(order) if self.reverse else order:
                self.part[b] = total
                total = total + self.got[b]
            return total

        def to_blocks(self):
            for offset in away:
                p = pair_at(offset)
                recv = pairs + 1 + (pairs - offset) % pairs
                for dy in (2, 1, 3, 0):
                    y = line_at(dy)
                    part = self.part.at[y * pairs + p]
                    if offset or dy:
                        self.copy(
                            part, self.back.at[pair, line], 2, recv, device(y, p, side)
                        ).start()
                    else:
                        self.back[pair, line] = self.part[y * pairs + p]

        def to_mate_back(self, offsets):
            second = side == (0 if self.reverse else 1)
            for offset in offsets:
                p = pair_at(offset)
                chunk = self.back.at[p] if offset else self.back.at[p, pl.ds(0, LINES - 1)]
                self.copy(chunk, chunk, 2, pairs + 1 + offset, mate).wait_recv()
                base = self.back[p]
                self.share[p] = base + jnp.where(second, 0.0, self.local[side, p])
                self.copy(
                    self.share.at[p], self.result.at[side, p], 3, 2 * pairs + 1, mate
                ).start()
                self.result[side, p] = base + jnp.where(second, self.other[p], 0.0)

        def finish(self):
            whole = self.result.at[0]
            self.copy(whole, whole, 3, 2 * pairs + 1, mate).wait_recv()

        def sent(self):
            whole = self.result.at[0]
            most = self.got.at[pl.ds(0, LINES * pairs - 1)]
            for send, ref in enumerate((whole, most, most, whole)):
                self.copy(ref, ref, send, 0, mate).wait_send()

    scan1 = Scan(local1, before, mate1, sums1, got1, part1, back1, share1, 0, False)
    scan2 = Scan(local2, after, mate2, sums2, got2, part2, back2, share2, 1, True)

    scan1.to_mate()
    forward_inside(1)
    scan1.to_owners()
    for h in range(heads):
        qt[h] = q[:, cols(h)].T
    forward_inside(2)
    scan1.add_up(state_ref[side * (n_seq // 2) + pair * LINES + line])
    scan1.to_blocks()
    forward_inside(3)
    scan1.to_mate_back(away[::-1])

    def gain_of(h):
        return gain_ref[h : h + 1, :]

    def forward_carried(part, squares, products):
        for i in range(heads // 2):
            h = heads // 2 * part + i
            at = pl.ds(pl.multiple_of(h * HEAD, HEAD), HEAD)
            high, low = halves(before[part, LINES * i : LINES * (i + 1)].reshape(HEAD, HEAD))
            a = att[:, at] + (nn(q[:, at], high) + nn(q[:, at], low))
            att[:, at] = a
            squares = squares + a * a
            products = products + a * (u[:, at].astype(F32) * gain_ref[pl.ds(h, 1), :])
        return squares, products

    nothing = jnp.zeros((tokens, HEAD), F32)
    squares, products = forward_carried(side, nothing, nothing)
    scan1.finish()
    squares, products = forward_carried(1 - side, squares, products)
    blocks = tokens // HEAD
    for j in range(blocks):
        rows_j = slice(j * HEAD, (j + 1) * HEAD)
        stats[mine, j : j + 1, :] = jnp.sum(squares[rows_j].T, axis=0, keepdims=True)
        stats[mine, blocks + j : blocks + j + 1, :] = jnp.sum(
            products[rows_j].T, axis=0, keepdims=True
        )
    for i in range(1, n_head):
        copy_to(
            stats.at[mine], stats.at[mine], send_sem.at[2], recv_sem.at[2],
            head=lax.rem(mine + i, n_head),
        ).start()
    others = stats.at[pl.ds(0, n_head - 1)]
    copy_to(others, others, send_sem.at[2], recv_sem.at[2], head=mine).wait_recv()
    total = stats[0]
    for i in range(1, n_head):
        total = total + stats[i]
    mean = total * (1.0 / (heads * HEAD * n_head))
    inverse = lax.rsqrt(mean[:blocks] + 1e-06)
    coef = mean[blocks:] * inverse * inverse

    def column(x, j):
        return jnp.broadcast_to(x[j : j + 1, :], (HEAD, HEAD)).T

    inverse = jnp.concatenate([column(inverse, j) for j in range(blocks)], axis=0)
    coef = jnp.concatenate([column(coef, j) for j in range(blocks)], axis=0)
    for h in range(heads):
        scaled = u[:, cols(h)].astype(F32) * gain_of(h)
        d = inverse * (scaled - att[:, cols(h)] * coef)
        d_low = d.astype(BF16)
        dfull[:, cols(h)] = d
        dlow[:, cols(h)] = d_low
        put_state(local2, h, nn(qt[h], d_low))
    scan2.to_mate()

    gains[0] = jnp.zeros((ROWS, HEAD), F32)
    for h in range(heads):
        normed = att[:, cols(h)] * inverse
        normed_out[:, cols(h)] = (normed * gain_of(h)).astype(BF16)
        gains[0, h : h + 1, :] = jnp.sum(
            u[:, cols(h)].astype(F32) * normed, axis=0, keepdims=True
        )

    to_mate = copy_to(gains.at[0], gains.at[3], send_sem.at[7], recv_sem.at[7], seq=mate)
    to_mate.start()
    scan2.to_owners()

    to_mate.wait_recv()
    gains[1] = gains[0] + gains[3]
    line_gains[pair] = gains[1]
    for offset in away[:-1]:
        copy_to(
            gains.at[1], line_gains.at[pair], send_sem.at[8], recv_sem.at[8],
            seq=device(line, pair_at(offset), side),
        ).start()

    def query_gradient(h):
        d_low = dlow[:, cols(h)]
        d_rest = (dfull[:, cols(h)] - d_low.astype(F32)).astype(BF16)
        high, low = halves(state_of(before, h))
        carried = nt(d_low, high) + (nt(d_low, low) + nt(d_rest, high))
        top, low = causal(d_low, v[:, cols(h)], k[:, cols(h)])
        qgrad_out[lo, cols(h)] = (top + carried[lo]).astype(BF16)
        qgrad_out[hi, cols(h)] = (low + carried[hi]).astype(BF16)

    for h in range(heads):
        query_gradient(h)

    totals[me] = scan2.add_up(jnp.zeros((ROWS, HEAD), F32))

    def send_total(j, carry):
        copy_to(
            totals.at[me], totals.at[me], send_sem.at[5], recv_sem.at[5],
            seq=line * PLANES + step_z(j),
        ).start()
        return carry

    scan2.to_blocks()
    lax.fori_loop(0, PLANES - 1, send_total, 0)

    for h in range(heads):
        top, low = anticausal(v[:, cols(h)], dlow[:, cols(h)], q[:, cols(h)])
        kpart[lo, cols(h)] = top
        kpart[hi, cols(h)] = low
        top, low = anticausal(k[:, cols(h)], q[:, cols(h)], dlow[:, cols(h)])
        vpart[lo, cols(h)] = top
        vpart[hi, cols(h)] = low

    scan2.to_mate_back(away[pairs // 2 :][::-1])
    some = totals.at[pl.ds(0, PLANES - 1)]
    copy_to(some, some, send_sem.at[5], recv_sem.at[5], seq=me).wait_recv()
    row = totals.at[pl.ds(line * PLANES, PLANES)]
    for i in (2, 1, 3):
        copy_to(
            row, row, send_sem.at[6], recv_sem.at[6], seq=device(line_at(i), pair, side)
        ).start()
    seven = line_gains.at[pl.ds(0, pairs - 1)]
    copy_to(seven, seven, send_sem.at[8], recv_sem.at[8], seq=me).wait_recv()
    gain = line_gains[0]
    for i in range(1, pairs):
        gain = gain + line_gains[i]
    gains[2] = gain
    all_gains[line] = gain
    for i in (2, 1, 3):
        copy_to(
            gains.at[2], all_gains.at[line], send_sem.at[9], recv_sem.at[9],
            seq=device(line_at(i), pair, side),
        ).start()

    def other_gradients(part):
        for i in range(heads // 2):
            at = pl.ds(pl.multiple_of((heads // 2 * part + i) * HEAD, HEAD), HEAD)
            rows_i = after[part, LINES * i : LINES * (i + 1)].reshape(HEAD, HEAD)
            high, low = halves(rows_i)
            vh, kh = v[:, at], k[:, at]
            kgrad_out[:, at] = (kpart[:, at] + (nt(vh, high) + nt(vh, low))).astype(BF16)
            vgrad_out[:, at] = (vpart[:, at] + (nn(kh, high) + nn(kh, low))).astype(BF16)

    scan2.to_mate_back(away[: pairs // 2][::-1])
    other_gradients(side)
    scan2.finish()
    other_gradients(1 - side)

    three = totals.at[pl.ds(0, (LINES - 1) * PLANES)]
    copy_to(three, three, send_sem.at[6], recv_sem.at[6], seq=me).wait_recv()
    for at in range(n_seq):
        owner = device(at % LINES, at % (n_seq // 2) // LINES, at // (n_seq // 2))
        state_out[at] = totals[owner]
    some_gains = all_gains.at[pl.ds(0, LINES - 1)]
    copy_to(some_gains, some_gains, send_sem.at[9], recv_sem.at[9], seq=me).wait_recv()
    gain = all_gains[0]
    for i in range(1, LINES):
        gain = gain + all_gains[i]
    gain_out[...] = gain[:heads]

    scan1.sent()
    scan2.sent()
    copy_to(others, others, send_sem.at[2], recv_sem.at[2], head=mine).wait_send()
    copy_to(some, some, send_sem.at[5], recv_sem.at[5], seq=me).wait_send()
    copy_to(three, three, send_sem.at[6], recv_sem.at[6], seq=me).wait_send()
    to_mate.wait_send()
    copy_to(seven, seven, send_sem.at[8], recv_sem.at[8], seq=me).wait_send()
    copy_to(some_gains, some_gains, send_sem.at[9], recv_sem.at[9], seq=me).wait_send()


def store_kernel(*refs):
    n = len(refs) // 2
    stores = []
    for i in range(n):
        cuts = 1
        rows = refs[i].shape[0] // cuts
        for c in range(cuts):
            at = pl.ds(c * rows, rows)
            stores.append(
                pltpu.make_async_copy(
                    refs[i].at[at], refs[n + i].at[at], refs[-1].at[len(stores)]
                )
            )
    for store in stores:
        store.start()
    for store in stores:
        store.wait()


def per_device(query_in, key_in, value_in, upstream, norm_gain, state_in):
    tokens, columns = query_in.shape
    heads = state_in.shape[0]
    n_seq = lax.axis_size("seq")
    n_head = lax.axis_size("head")
    wide = jax.ShapeDtypeStruct((tokens, columns), BF16)
    slices = (n_seq, ROWS, HEAD)
    vmem = pl.BlockSpec(memory_space=pltpu.VMEM)
    anywhere = pl.BlockSpec(memory_space=pl.ANY)
    hbm = pl.BlockSpec(memory_space=pltpu.HBM)
    low = pltpu.VMEM((tokens, columns), BF16)
    full = pltpu.VMEM((tokens, columns), F32)
    pairs = PLANES // 2
    whole = pltpu.VMEM((2, pairs, LINES, ROWS, HEAD), F32)
    half = pltpu.VMEM((pairs, LINES, ROWS, HEAD), F32)
    flat = pltpu.VMEM((pairs * LINES, ROWS, HEAD), F32)
    shapes = (
        wide, wide, wide, wide,
        jax.ShapeDtypeStruct((heads, HEAD), F32),
        jax.ShapeDtypeStruct(slices, F32),
    )
    outs = pl.pallas_call(
        kernel,
        name="attention_and_gradients",
        out_shape=shapes,
        in_specs=[hbm] * 6,
        out_specs=[vmem] * 6,
        scratch_shapes=[low] * 4
        + [pltpu.VMEM((heads, HEAD), F32), pltpu.VMEM(slices, F32)]
        + [pltpu.VMEM((heads, HEAD, tokens), BF16), full, full, low, full, full]
        + ([whole] * 2 + [half] * 2 + [flat] * 2 + [half] * 2) * 2
        + [
            pltpu.VMEM((n_head, ROWS, HEAD), F32),
            pltpu.VMEM(slices, F32),
            pltpu.VMEM((4, ROWS, HEAD), F32),
            pltpu.VMEM((pairs, ROWS, HEAD), F32),
            pltpu.VMEM((LINES, ROWS, HEAD), F32),
            pltpu.SemaphoreType.DMA((6,)),
            pltpu.SemaphoreType.DMA((10,)),
            pltpu.SemaphoreType.DMA((10,)),
            pltpu.SemaphoreType.DMA((8,)),
            pltpu.SemaphoreType.DMA((2 * (2 * pairs + 2),)),
        ],
        compiler_params=pltpu.CompilerParams(
            collective_id=0, has_side_effects=True, vmem_limit_bytes=51 << 20
        ),
    )(
        *(
            pltpu.with_memory_space_constraint(x, pltpu.HBM)
            for x in (
                query_in, key_in, value_in, upstream,
                norm_gain.reshape(heads, HEAD), state_in.reshape(slices),
            )
        )
    )
    outs = pl.pallas_call(
        store_kernel,
        name="store",
        out_shape=shapes,
        in_specs=[anywhere] * 6,
        out_specs=[hbm] * 6,
        scratch_shapes=[pltpu.SemaphoreType.DMA((6,))],
        compiler_params=pltpu.CompilerParams(vmem_limit_bytes=1 << 20),
    )(*outs)
    return (
        outs[0], outs[1], outs[2], outs[3],
        outs[4].reshape(heads * HEAD), outs[5].reshape(state_in.shape),
    )


def solution(mesh):
    wide = P("seq", "head")
    return jax.shard_map(
        per_device,
        mesh=mesh,
        in_specs=(wide, wide, wide, wide, P("head"), P("head", None, None)),
        out_specs=(wide, wide, wide, wide, P("head"), P("head", None, None)),
        check_vma=False,
    )
```
